256 devices in a mesh: dp: 16 (over z, core), seq: 16 (over y, x).
Axes of the slice: x: 4, y: 4, z: 8, core: 2. Of those that a mesh axis runs over, the one named last changes fastest.
Arguments:
- queries: bfloat16 [65536, 3584], P(('dp', 'seq')), may hold values from -25 to 25
- key_states: bfloat16 [65536, 512], P(('dp', 'seq')), may hold values from -6 to 6
- value_vectors: bfloat16 [65536, 512], P(('dp', 'seq')), may hold values from -6 to 6
- segment_ids: int32 [65536], P(('dp', 'seq')), may hold values from 0 to 156, as said below
Outputs:
- attended: bfloat16 [65536, 3584], P(('dp', 'seq'))
The draws below stay inside these ranges and needn't reach their ends.
Inputs may be any that keep to these rules, and one draw needn't show every extreme that they name: `segment_ids`: segment ids never fall along the token order and take every value from min to max; the tokens of one segment lie within 9 consecutive blocks of 256 tokens, and in every draw some segment spans exactly 9 such blocks.
All inputs are finite; a program needn't handle non-finite values.
Results may differ from the reference program's by a relative error of at most 0.0031.
Values may be sent and summed in bfloat16 or wider, within the bound.
No kernel may reach another device: no remote copies, remote signals or barrier semaphores. Data moves between devices by JAX's collectives and lax.ppermute only.
A program may use at most 192 MiB of HBM per device.

```python
import jax
import jax.numpy as jnp
from jax import lax

QUERY_HEAD_COUNT = 28
KEY_VALUE_HEADS = 4
HEAD_WIDTH = 128
TOK_DEV = 256
REACH = 8
TOKEN_TOTAL = 65536


def draw_queries(key, part):
    key = jax.random.fold_in(key, 11)
    noise_key = jax.random.fold_in(key, 0)
    random_perturbation = jnp.clip(jax.random.normal(noise_key, (TOKEN_TOTAL, QUERY_HEAD_COUNT * HEAD_WIDTH), jnp.float32), -6.0, 6.0)
    attention_output = 2.0 * random_perturbation
    return attention_output.astype(jnp.bfloat16)


def draw_key_states(key, part):
    key = jax.random.fold_in(key, 23)
    random_perturbation = jnp.clip(jax.random.normal(key, (TOKEN_TOTAL, KEY_VALUE_HEADS * HEAD_WIDTH), jnp.float32), -6.0, 6.0)
    attention_output = random_perturbation
    return attention_output.astype(jnp.bfloat16)


def draw_segment_ids(key, part):
    key = jax.random.fold_in(key, 37)
    offset_key, pick_key, length_key = jax.random.split(key, 3)
    frame_len = REACH * TOK_DEV
    frame_count = TOKEN_TOTAL // frame_len
    offsets = jax.random.randint(offset_key, (frame_count,), TOK_DEV // 4, 3 * TOK_DEV // 4, dtype=jnp.int32)
    frame_starts = jnp.arange(frame_count, dtype=jnp.int32) * frame_len + offsets
    chosen = jax.random.randint(pick_key, (), 0, frame_count - 1, dtype=jnp.int32)
    frame_ends = jnp.concatenate([frame_starts[1:], jnp.full((1,), TOKEN_TOTAL, jnp.int32)])
    short_lens = TOK_DEV // 2 + jax.random.randint(length_key, (frame_count, 4), 0, TOK_DEV // 2, dtype=jnp.int32)
    tails = jnp.cumsum(short_lens[:, ::-1], axis=1)[:, ::-1].astype(jnp.int32)
    cuts = frame_ends[:, None] - tails
    is_long = jnp.arange(frame_count, dtype=jnp.int32) == chosen
    cuts = jnp.where(is_long[:, None], frame_starts[:, None], cuts)
    marks = jnp.zeros((TOKEN_TOTAL,), jnp.int32).at[0].set(1)
    marks = marks.at[frame_starts].set(1)
    marks = marks.at[cuts.reshape(-1)].set(1)
    return (jnp.cumsum(marks) - 1).astype(jnp.int32)


def shard_levels(key, dims, shards, low, top_value):
    def one(dim, parts):
        draws = jax.random.uniform(jax.random.fold_in(jax.random.fold_in(key, 6), dim), (parts,), jnp.float32, low / len(shards), top_value / len(shards))
        return jnp.repeat(jnp.exp(draws), dims[dim] // parts).reshape((-1,) + (1,) * (len(dims) - dim - 1))

    level = one(*shards[0])
    for cut in shards[1:]:
        level = level * one(*cut)
    return level


def normal_values(stream_key, shape, scale, reach, pieces=(), kind=jnp.bfloat16):
    gain = shard_levels(stream_key, shape, pieces, -0.22, 0.18) if pieces else 1.0
    values = jax.random.normal(stream_key, shape, jnp.float32) * scale * gain
    return jnp.minimum(jnp.maximum(values, -reach), reach).astype(kind)


def setup_inputs(seed: int = 0) -> dict:
    splits = jax.random.split(jax.random.key(seed), 5)
    return {
        "queries": draw_queries(jax.random.fold_in(splits[4], 71), 0),
        "key_states": draw_key_states(jax.random.fold_in(splits[4], 71), 0),
        "value_vectors": normal_values(splits[2], (TOKEN_TOTAL, KEY_VALUE_HEADS * HEAD_WIDTH), 1.0, 6.0, ((0, 256),)),
        "segment_ids": draw_segment_ids(jax.random.fold_in(splits[4], 71), 0),
    }


def attend_block(query_block, key_window, value_window, allowed):
    queries_per_group = QUERY_HEAD_COUNT // KEY_VALUE_HEADS
    row_count = query_block.shape[0]
    scaling = 1.0 / (HEAD_WIDTH ** 0.5)
    outputs = []
    for current_head in range(KEY_VALUE_HEADS):
        query_heads = query_block[:, current_head * queries_per_group * HEAD_WIDTH:(current_head + 1) * queries_per_group * HEAD_WIDTH]
        query_heads = query_heads.astype(jnp.float32).reshape(row_count, queries_per_group, HEAD_WIDTH)
        key_head = key_window[:, current_head * HEAD_WIDTH:(current_head + 1) * HEAD_WIDTH].astype(jnp.float32)
        value_head = value_window[:, current_head * HEAD_WIDTH:(current_head + 1) * HEAD_WIDTH].astype(jnp.float32)
        scores = jnp.einsum("tgd,sd->gts", query_heads, key_head) * scaling
        scores = jnp.where(allowed[None], scores, -jnp.inf)
        largest = jnp.max(scores, axis=2, keepdims=True)
        weights = jnp.exp(scores - largest)
        totals = jnp.sum(weights, axis=2, keepdims=True)
        probabilities = lax.optimization_barrier(weights.astype(jnp.bfloat16)).astype(jnp.float32)
        mixture = jnp.einsum("gts,sd->tgd", probabilities, value_head)
        mixture = mixture / jnp.transpose(totals, (1, 0, 2))
        outputs.append(mixture.reshape(row_count, queries_per_group * HEAD_WIDTH))
    return jnp.concatenate(outputs, axis=1).astype(jnp.bfloat16)


def reference(queries, key_states, value_vectors, segment_ids):
    padding = REACH * TOK_DEV
    key_value_width = KEY_VALUE_HEADS * HEAD_WIDTH
    key_padded = jnp.concatenate([jnp.zeros((padding, key_value_width), jnp.bfloat16), key_states], axis=0)
    value_padded = jnp.concatenate([jnp.zeros((padding, key_value_width), jnp.bfloat16), value_vectors], axis=0)
    segment_padded = jnp.concatenate([-jnp.ones((padding,), jnp.int32), segment_ids], axis=0)
    block_count = TOKEN_TOTAL // TOK_DEV

    def one_block(block_index):
        first_row = (block_index * TOK_DEV).astype(jnp.int32)
        query_block = lax.dynamic_slice_in_dim(queries, first_row, TOK_DEV, 0)
        key_window = lax.dynamic_slice_in_dim(key_padded, first_row, padding + TOK_DEV, 0)
        value_window = lax.dynamic_slice_in_dim(value_padded, first_row, padding + TOK_DEV, 0)
        segment_query = lax.dynamic_slice_in_dim(segment_ids, first_row, TOK_DEV, 0)
        segment_window = lax.dynamic_slice_in_dim(segment_padded, first_row, padding + TOK_DEV, 0)
        query_place = first_row + jnp.arange(TOK_DEV, dtype=jnp.int32)
        window_place = first_row - padding + jnp.arange(padding + TOK_DEV, dtype=jnp.int32)
        allowed = (segment_query[:, None] == segment_window[None, :]) & (window_place[None, :] <= query_place[:, None]) & (window_place[None, :] >= 0)
        return attend_block(query_block, key_window, value_window, allowed)

    blocks = lax.map(one_block, jnp.arange(block_count, dtype=jnp.int32))
    return blocks.reshape(TOKEN_TOTAL, QUERY_HEAD_COUNT * HEAD_WIDTH)
```

```python
import functools

import jax
import jax.numpy as jnp
from jax import lax
from jax.experimental import pallas as pl
from jax.experimental.pallas import tpu as pltpu
from jax.sharding import PartitionSpec as P

KEY_VALUE_HEADS = 4
GROUP = 7
WIDTH = 128
TOKENS = 256
EXTRA = 16
ROWS = 2 * TOKENS + EXTRA
AXES = ("dp", "seq")
SCALE = 1.4426950408889634 / WIDTH**0.5
LOW, HIGH = 1e-25, 1e30
NT = (((1,), (1,)), ((), ()))
NN = (((1,), (0,)), ((), ()))


def rank_of(plane, y, x):
    return (plane * 4 + y) * 4 + x


def turned_along_x(value, steps):
    pairs = [
        (rank_of(plane, y, x), rank_of(plane, y, (x + steps) % 4))
        for plane in range(16)
        for y in range(4)
        for x in range(4)
    ]
    return lax.ppermute(value, AXES, pairs)


def shifted(value, steps):
    return lax.ppermute(value, AXES, [(r, r + steps) for r in range(256 - steps)])


def ids_down(rows):
    halves = [
        jnp.transpose(jnp.broadcast_to(rows[i : i + 1], (WIDTH, WIDTH))) for i in range(2)
    ]
    return jnp.concatenate(halves, axis=0)


def ids_across(rows, count):
    halves = [jnp.broadcast_to(rows[i : i + 1], (count, WIDTH)) for i in range(2)]
    return jnp.concatenate(halves, axis=1)


def ids_of(block):
    return block[2 * TOKENS : ROWS, :].astype(jnp.float32)[0:2]


def general_head(head, whole, q_ref, o_ref, held, top, total, mix, sem):
    count = len(whole)
    for b in range(count):
        columns = pl.ds(pl.multiple_of(head * WIDTH, WIDTH), WIDTH)
        copy = pltpu.make_async_copy(whole[b].at[:, columns], held.at[b], sem)
        copy.start()
        copy.wait()
    mine = ids_down(ids_of(held[count - 1]))
    mine = jnp.concatenate([mine, mine], axis=1)
    later = lax.broadcasted_iota(jnp.int32, (TOKENS, TOKENS), 1) > lax.broadcasted_iota(
        jnp.int32, (TOKENS, TOKENS), 0
    )

    @pl.loop(0, GROUP)
    def _(g):
        columns = pl.ds(pl.multiple_of(g * WIDTH, WIDTH), WIDTH)
        top[...] = jnp.full((TOKENS, WIDTH), -1e30, jnp.float32)
        total[...] = jnp.zeros((TOKENS, WIDTH), jnp.float32)
        mix[...] = jnp.zeros((TOKENS, WIDTH), jnp.float32)

        @pl.loop(0, count)
        def _(b):
            s = lax.dot_general(
                q_ref[:, columns], held[b, 0:TOKENS, :], NT, preferred_element_type=jnp.float32
            )
            s = s * SCALE
            theirs = ids_across(
                held[b, 2 * TOKENS : ROWS, :].astype(jnp.float32)[0:2], TOKENS
            )
            allowed = (mine == theirs) & ~(later & (b == count - 1))
            s = jnp.where(allowed, s, -1e30)
            now = jnp.maximum(top[:, 0:1], jnp.max(s, axis=1, keepdims=True))
            p = jnp.where(allowed, jnp.exp2(s - now), 0.0)
            keep = jnp.exp2(top[:, 0:1] - now)
            total[...] = total[...] * keep + jnp.sum(p, axis=1, keepdims=True)
            mix[...] = mix[...] * keep + lax.dot_general(
                p.astype(jnp.bfloat16),
                held[b, TOKENS : 2 * TOKENS, :],
                NN,
                preferred_element_type=jnp.float32,
            )
            top[...] = jnp.broadcast_to(now, (TOKENS, WIDTH))

        o_ref[:, columns] = (mix[...] / total[...]).astype(jnp.bfloat16)


def attend(count, q_ref, *refs):
    blocks = refs[:count]
    whole = refs[count : 2 * count]
    o_ref = refs[2 * count]
    mixed, picked, causal, rows_in, held, top, total, mix, sem = refs[2 * count + 1 :]
    head = pl.program_id(0)
    own = blocks[-1]

    @pl.when(head == 0)
    def _():
        ids = ids_of(own)
        down = ids_down(ids)
        first = ids[0:1, 0:1]
        rows_in[...] = jnp.where(down == first, 1.0, 0.0)
        down = jnp.concatenate([down, down], axis=1)
        row = lax.broadcasted_iota(jnp.int32, (TOKENS, TOKENS), 0)
        column = lax.broadcasted_iota(jnp.int32, (TOKENS, TOKENS), 1)
        causal[...] = jnp.where((down == ids_across(ids, TOKENS)) & (column <= row), 1.0, 0.0)
        for b in range(count - 1):
            picked[b] = ids_down(jnp.where(ids_of(blocks[b]) == first, 1.0, 0.0)).astype(
                jnp.bfloat16
            )

    for b in range(count):
        mask = picked[b] if b < count - 1 else jnp.ones((TOKENS, WIDTH), jnp.bfloat16)
        values = blocks[b][TOKENS : 2 * TOKENS, :]
        mixed[b, :, 0:WIDTH] = values * mask if b < count - 1 else values
        mixed[b, :, WIDTH:] = mask

    good = None
    for g in range(GROUP):
        columns = slice(g * WIDTH, (g + 1) * WIDTH)
        q = q_ref[:, columns]
        sums = None
        for b in range(count):
            s = lax.dot_general(
                q, blocks[b][0:TOKENS, :], NT, preferred_element_type=jnp.float32
            )
            p = jnp.exp2(s * SCALE)
            if b == count - 1:
                p = p * causal[...]
                inside = rows_in[...] > 0.5
                sums = jnp.where(jnp.concatenate([inside, inside], axis=1), sums, 0.0)
            term = lax.dot_general(
                p.astype(jnp.bfloat16), mixed[b], NN, preferred_element_type=jnp.float32
            )
            sums = term if b == 0 else sums + term
        weight = sums[:, WIDTH:]
        o_ref[:, columns] = (sums[:, :WIDTH] / weight).astype(jnp.bfloat16)
        fine = jnp.where((weight > LOW) & (weight < HIGH), 1.0, 0.0)
        good = fine if good is None else jnp.minimum(good, fine)

    @pl.when(jnp.min(good) < 0.5)
    def _():
        general_head(head, whole, q_ref, o_ref, held, top, total, mix, sem)


def attention(queries, blocks):
    count = len(blocks)
    by_head = lambda rows, columns: pl.BlockSpec((rows, columns), lambda h: (0, h))
    return pl.pallas_call(
        functools.partial(attend, count),
        grid=(KEY_VALUE_HEADS,),
        in_specs=[by_head(TOKENS, GROUP * WIDTH)]
        + [by_head(ROWS, WIDTH)] * count
        + [pl.BlockSpec(memory_space=pl.ANY)] * count,
        out_specs=by_head(TOKENS, GROUP * WIDTH),
        out_shape=jax.ShapeDtypeStruct(queries.shape, jnp.bfloat16),
        scratch_shapes=[
            pltpu.VMEM((count, TOKENS, 2 * WIDTH), jnp.bfloat16),
            pltpu.VMEM((count - 1, TOKENS, WIDTH), jnp.bfloat16),
            pltpu.VMEM((TOKENS, TOKENS), jnp.float32),
            pltpu.VMEM((TOKENS, WIDTH), jnp.float32),
            pltpu.VMEM((count, ROWS, WIDTH), jnp.bfloat16),
            pltpu.VMEM((TOKENS, WIDTH), jnp.float32),
            pltpu.VMEM((TOKENS, WIDTH), jnp.float32),
            pltpu.VMEM((TOKENS, WIDTH), jnp.float32),
            pltpu.SemaphoreType.DMA,
        ],
        compiler_params=pltpu.CompilerParams(vmem_limit_bytes=56 * 1024 * 1024),
        cost_estimate=pl.CostEstimate(
            flops=28 * 256 * 256 * count * 512,
            bytes_accessed=4_000_000 + count * 540_000,
            transcendentals=28 * 256 * 256 * count,
        ),
    )(queries, *blocks, *blocks)


def per_device(queries, key_states, value_vectors, segment_ids):
    ids = (segment_ids + 1).astype(jnp.bfloat16).reshape(2, WIDTH)
    ids = jnp.pad(jnp.tile(ids, (1, KEY_VALUE_HEADS)), ((0, EXTRA - 2), (0, 0)))
    own = jnp.concatenate([key_states, value_vectors, ids], axis=0)
    x = lax.axis_index("seq") % 4
    four = shifted(own, 4)
    eight = shifted(own, 8)
    middle = [turned_along_x(four, a) for a in (1, 3)]
    ends = [turned_along_x(jnp.where(x + a < 4, own, eight), a) for a in (1, 3)]
    two = turned_along_x(jnp.where(x < 2, own, four), 2)
    six = shifted(two, 4)
    return attention(queries, [four, eight, *middle, *ends, two, six, own])


def solution(mesh):
    rows = P(AXES, None)
    return jax.shard_map(
        per_device,
        mesh=mesh,
        in_specs=(rows, rows, rows, P(AXES)),
        out_specs=rows,
        check_vma=False,
    )
```

```python
import functools

import jax
import jax.numpy as jnp
from jax import lax
from jax.experimental import pallas as pl
from jax.experimental.pallas import tpu as pltpu
from jax.sharding import PartitionSpec as P

KEY_VALUE_HEADS = 4
GROUP = 7
WIDTH = 128
TOKENS = 256
EXTRA = 16
ROWS = 2 * TOKENS + EXTRA
AXES = ("dp", "seq")
SCALE = 1.4426950408889634 / WIDTH**0.5
LOW, HIGH = 1e-25, 1e30
VMEM_LIMIT = 60 * 1024 * 1024
NT = (((1,), (1,)), ((), ()))
NN = (((1,), (0,)), ((), ()))


def rank_of(plane, y, x):
    return (plane * 4 + y) * 4 + x


def turned_along_x(value, steps):
    pairs = [
        (rank_of(plane, y, x), rank_of(plane, y, (x + steps) % 4))
        for plane in range(16)
        for y in range(4)
        for x in range(4)
    ]
    return lax.ppermute(value, AXES, pairs)


def turned_along_y(value, steps):
    pairs = [
        (rank_of(plane, y, x), rank_of(plane, (y + steps) % 4, x))
        for plane in range(16)
        for y in range(4)
        for x in range(4)
    ]
    return lax.ppermute(value, AXES, pairs)


def two_rows_on(value):
    pairs = [
        (rank_of(plane, (y - 1) % 4, x), rank_of(plane, y, x) + 8)
        for plane in range(16)
        for y in range(4)
        for x in range(4)
        if rank_of(plane, y, x) + 8 < 256
    ]
    return lax.ppermute(value, AXES, pairs)


def shifted(value, steps):
    return lax.ppermute(value, AXES, [(r, r + steps) for r in range(256 - steps)])


def ids_down(rows):
    halves = [
        jnp.transpose(jnp.broadcast_to(rows[i : i + 1], (WIDTH, WIDTH))) for i in range(2)
    ]
    return jnp.concatenate(halves, axis=0)


def ids_across(rows, count):
    halves = [jnp.broadcast_to(rows[i : i + 1], (count, WIDTH)) for i in range(2)]
    return jnp.concatenate(halves, axis=1)


def ids_of(block):
    return block[2 * TOKENS : ROWS, :].astype(jnp.float32)[0:2]


def general_head(head, whole, q_ref, o_ref, held, top, total, mix, sem):
    count = len(whole)
    for b in range(count):
        columns = pl.ds(pl.multiple_of(head * WIDTH, WIDTH), WIDTH)
        copy = pltpu.make_async_copy(whole[b].at[:, columns], held.at[b], sem)
        copy.start()
        copy.wait()
    mine = ids_down(ids_of(held[count - 1]))
    mine = jnp.concatenate([mine, mine], axis=1)
    later = lax.broadcasted_iota(jnp.int32, (TOKENS, TOKENS), 1) > lax.broadcasted_iota(
        jnp.int32, (TOKENS, TOKENS), 0
    )

    @pl.loop(0, GROUP)
    def _(g):
        columns = pl.ds(pl.multiple_of(g * WIDTH, WIDTH), WIDTH)
        top[...] = jnp.full((TOKENS, WIDTH), -1e30, jnp.float32)
        total[...] = jnp.zeros((TOKENS, WIDTH), jnp.float32)
        mix[...] = jnp.zeros((TOKENS, WIDTH), jnp.float32)

        @pl.loop(0, count)
        def _(b):
            s = lax.dot_general(
                q_ref[:, columns], held[b, 0:TOKENS, :], NT, preferred_element_type=jnp.float32
            )
            s = s * SCALE
            theirs = ids_across(
                held[b, 2 * TOKENS : ROWS, :].astype(jnp.float32)[0:2], TOKENS
            )
            allowed = (mine == theirs) & ~(later & (b == count - 1))
            s = jnp.where(allowed, s, -1e30)
            now = jnp.maximum(top[:, 0:1], jnp.max(s, axis=1, keepdims=True))
            p = jnp.where(allowed, jnp.exp2(s - now), 0.0)
            keep = jnp.exp2(top[:, 0:1] - now)
            total[...] = total[...] * keep + jnp.sum(p, axis=1, keepdims=True)
            mix[...] = mix[...] * keep + lax.dot_general(
                p.astype(jnp.bfloat16),
                held[b, TOKENS : 2 * TOKENS, :],
                NN,
                preferred_element_type=jnp.float32,
            )
            top[...] = jnp.broadcast_to(now, (TOKENS, WIDTH))

        o_ref[:, columns] = (mix[...] / total[...]).astype(jnp.bfloat16)


def attend(prior, has_own, has_before, last, whole_count, q_ref, own, *refs):
    refs = list(refs)
    take = lambda n: [refs.pop(0) for _ in range(n)]
    blocks = take(prior)
    before = take(2) if has_before else None
    whole = take(whole_count)
    outs = take(1 if last else 2)
    mixed, picked, causal, rows_in = take(4)
    head = pl.program_id(0)
    count = prior + has_own

    @pl.when(head == 0)
    def _():
        ids = ids_of(own)
        down = ids_down(ids)
        first = ids[0:1, 0:1]
        rows_in[...] = jnp.where(down == first, 1.0, 0.0)
        if has_own:
            down = jnp.concatenate([down, down], axis=1)
            row = lax.broadcasted_iota(jnp.int32, (TOKENS, TOKENS), 0)
            column = lax.broadcasted_iota(jnp.int32, (TOKENS, TOKENS), 1)
            same = down == ids_across(ids, TOKENS)
            causal[...] = jnp.where(same & (column <= row), 1.0, 0.0)
        for b in range(prior):
            picked[b] = ids_down(jnp.where(ids_of(blocks[b]) == first, 1.0, 0.0)).astype(
                jnp.bfloat16
            )

    for b in range(prior):
        mixed[b, :, 0:WIDTH] = blocks[b][TOKENS : 2 * TOKENS, :] * picked[b]
        mixed[b, :, WIDTH:] = picked[b]
    if has_own:
        mixed[prior, :, 0:WIDTH] = own[TOKENS : 2 * TOKENS, :]
        mixed[prior, :, WIDTH:] = jnp.ones((TOKENS, WIDTH), jnp.bfloat16)

    def term(q, keys, b, mask=None):
        s = lax.dot_general(q, keys, NT, preferred_element_type=jnp.float32)
        p = jnp.exp2(s * SCALE)
        if mask is not None:
            p = p * mask
        return lax.dot_general(
            p.astype(jnp.bfloat16), mixed[b], NN, preferred_element_type=jnp.float32
        )

    good = None
    weights = None
    lane = lax.broadcasted_iota(jnp.int32, (TOKENS, WIDTH), 1)
    for g in range(GROUP):
        columns = slice(g * WIDTH, (g + 1) * WIDTH)
        q = q_ref[:, columns]
        sums = term(q, blocks[0][0:TOKENS, :], 0)
        for b in range(1, prior):
            sums = sums + term(q, blocks[b][0:TOKENS, :], b)
        inside = rows_in[...] > 0.5
        mix = jnp.where(inside, sums[:, :WIDTH], 0.0)
        weight = jnp.where(inside, sums[:, WIDTH:], 0.0)
        if has_own:
            sums = term(q, own[0:TOKENS, :], prior, causal[...])
            mix = mix + sums[:, :WIDTH]
            weight = weight + sums[:, WIDTH:]
        if has_before:
            mix = mix + before[0][:, columns]
            weight = weight + before[1][:, g : g + 1]
        if last:
            outs[0][:, columns] = (mix / weight).astype(jnp.bfloat16)
            fine = jnp.where((weight > LOW) & (weight < HIGH), 1.0, 0.0)
            good = fine if good is None else jnp.minimum(good, fine)
        else:
            outs[0][:, columns] = mix
            weights = weight if weights is None else jnp.where(lane == g, weight, weights)
    if last:

        @pl.when(jnp.min(good) < 0.5)
        def _():
            general_head(head, whole, q_ref, outs[0], *refs)
    else:
        outs[1][...] = weights


def attention(queries, own, blocks, has_own, before, whole, last):
    by_head = lambda rows, columns: pl.BlockSpec((rows, columns), lambda h: (0, h))
    count = len(blocks) + has_own
    wide, narrow = by_head(TOKENS, GROUP * WIDTH), by_head(TOKENS, WIDTH)
    before_specs = [wide, narrow] if before else []
    if last:
        out_specs = wide
        out_shape = jax.ShapeDtypeStruct(queries.shape, jnp.bfloat16)
    else:
        out_specs = [wide, narrow]
        out_shape = [
            jax.ShapeDtypeStruct(queries.shape, jnp.float32),
            jax.ShapeDtypeStruct((TOKENS, KEY_VALUE_HEADS * WIDTH), jnp.float32),
        ]
    scratch = [
        pltpu.VMEM((count, TOKENS, 2 * WIDTH), jnp.bfloat16),
        pltpu.VMEM((len(blocks), TOKENS, WIDTH), jnp.bfloat16),
        pltpu.VMEM((TOKENS, TOKENS), jnp.float32),
        pltpu.VMEM((TOKENS, WIDTH), jnp.float32),
    ]
    if last:
        scratch += [
            pltpu.VMEM((len(whole), ROWS, WIDTH), jnp.bfloat16),
            pltpu.VMEM((TOKENS, WIDTH), jnp.float32),
            pltpu.VMEM((TOKENS, WIDTH), jnp.float32),
            pltpu.VMEM((TOKENS, WIDTH), jnp.float32),
            pltpu.SemaphoreType.DMA,
        ]
    return pl.pallas_call(
        functools.partial(attend, len(blocks), has_own, bool(before), last, len(whole)),
        grid=(KEY_VALUE_HEADS,),
        in_specs=[wide]
        + [by_head(ROWS, WIDTH)] * (1 + len(blocks))
        + before_specs
        + [pl.BlockSpec(memory_space=pl.ANY)] * len(whole),
        out_specs=out_specs,
        out_shape=out_shape,
        scratch_shapes=scratch,
        compiler_params=pltpu.CompilerParams(vmem_limit_bytes=VMEM_LIMIT),
        cost_estimate=pl.CostEstimate(
            flops=28 * 256 * 256 * count * 1024,
            bytes_accessed=4_000_000 + count * 540_000,
            transcendentals=28 * 256 * 256 * count,
        ),
    )(queries, own, *blocks, *before, *whole)


def per_device(queries, key_states, value_vectors, segment_ids):
    ids = (segment_ids + 1).astype(jnp.bfloat16).reshape(2, WIDTH)
    ids = jnp.pad(jnp.tile(ids, (1, KEY_VALUE_HEADS)), ((0, EXTRA - 2), (0, 0)))
    own = jnp.concatenate([key_states, value_vectors, ids], axis=0)
    x = lax.axis_index("seq") % 4
    four = shifted(own, 4)
    two = shifted(own, 2)
    eight = two_rows_on(turned_along_y(own, -1))
    middle = [turned_along_x(four, a) for a in (1, 3)]
    six = shifted(two, 4)
    ends = [turned_along_x(jnp.where(x + a < 4, own, eight), a) for a in (1, 3)]
    stage = attention(queries, own, [four, two], True, [], [], False)
    stage = attention(queries, own, [eight, *middle], False, stage, [], False)
    whole = [four, two, eight, *middle, six, *ends, own]
    return attention(queries, own, [six, *ends], False, stage, whole, True)


def solution(mesh):
    rows = P(AXES, None)
    return jax.shard_map(
        per_device,
        mesh=mesh,
        in_specs=(rows, rows, rows, P(AXES)),
        out_specs=rows,
        check_vma=False,
    )
```

```python
import functools

import jax
import jax.numpy as jnp
from jax import lax
from jax.experimental import pallas as pl
from jax.experimental.pallas import tpu as pltpu
from jax.sharding import PartitionSpec as P

KEY_VALUE_HEADS = 4
GROUP = 7
WIDTH = 128
TOKENS = 256
EXTRA = 16
ROWS = 2 * TOKENS + EXTRA
AXES = ("dp", "seq")
SCALE = 1.4426950408889634 / WIDTH**0.5
LOW, HIGH = 1e-25, 1e30
VMEM_LIMIT = 24 * 1024 * 1024
NT = (((1,), (1,)), ((), ()))
NN = (((1,), (0,)), ((), ()))


def rank_of(plane, y, x):
    return (plane * 4 + y) * 4 + x


def turned_along_x(value, steps):
    pairs = [
        (rank_of(plane, y, x), rank_of(plane, y, (x + steps) % 4))
        for plane in range(16)
        for y in range(4)
        for x in range(4)
    ]
    return lax.ppermute(value, AXES, pairs)


def turned_along_y(value, steps):
    pairs = [
        (rank_of(plane, y, x), rank_of(plane, (y + steps) % 4, x))
        for plane in range(16)
        for y in range(4)
        for x in range(4)
    ]
    return lax.ppermute(value, AXES, pairs)


def two_rows_on(value):
    pairs = [
        (rank_of(plane, (y - 1) % 4, x), rank_of(plane, y, x) + 8)
        for plane in range(16)
        for y in range(4)
        for x in range(4)
        if rank_of(plane, y, x) + 8 < 256
    ]
    return lax.ppermute(value, AXES, pairs)


def row_on(value, columns=range(4)):
    return lax.ppermute(value, AXES, [(r, r + 4) for r in range(252) if r % 4 in columns])


def ids_down(rows):
    halves = [
        jnp.transpose(jnp.broadcast_to(rows[i : i + 1], (WIDTH, WIDTH))) for i in range(2)
    ]
    return jnp.concatenate(halves, axis=0)


def ids_across(rows, count):
    halves = [jnp.broadcast_to(rows[i : i + 1], (count, WIDTH)) for i in range(2)]
    return jnp.concatenate(halves, axis=1)


def ids_of(block):
    return block[2 * TOKENS : ROWS, :].astype(jnp.float32)[0:2]


def general_head(head, whole, q_ref, o_ref, held, top, total, mix, sem):
    count = len(whole)
    for b in range(count):
        columns = pl.ds(pl.multiple_of(head * WIDTH, WIDTH), WIDTH)
        copy = pltpu.make_async_copy(whole[b].at[:, columns], held.at[b], sem)
        copy.start()
        copy.wait()
    mine = ids_down(ids_of(held[count - 1]))
    mine = jnp.concatenate([mine, mine], axis=1)
    later = lax.broadcasted_iota(jnp.int32, (TOKENS, TOKENS), 1) > lax.broadcasted_iota(
        jnp.int32, (TOKENS, TOKENS), 0
    )

    @pl.loop(0, GROUP)
    def _(g):
        columns = pl.ds(pl.multiple_of(g * WIDTH, WIDTH), WIDTH)
        top[...] = jnp.full((TOKENS, WIDTH), -1e30, jnp.float32)
        total[...] = jnp.zeros((TOKENS, WIDTH), jnp.float32)
        mix[...] = jnp.zeros((TOKENS, WIDTH), jnp.float32)

        @pl.loop(0, count)
        def _(b):
            s = lax.dot_general(
                q_ref[:, columns], held[b, 0:TOKENS, :], NT, preferred_element_type=jnp.float32
            )
            s = s * SCALE
            theirs = ids_across(
                held[b, 2 * TOKENS : ROWS, :].astype(jnp.float32)[0:2], TOKENS
            )
            allowed = (mine == theirs) & ~(later & (b == count - 1))
            s = jnp.where(allowed, s, -1e30)
            now = jnp.maximum(top[:, 0:1], jnp.max(s, axis=1, keepdims=True))
            p = jnp.where(allowed, jnp.exp2(s - now), 0.0)
            keep = jnp.exp2(top[:, 0:1] - now)
            total[...] = total[...] * keep + jnp.sum(p, axis=1, keepdims=True)
            mix[...] = mix[...] * keep + lax.dot_general(
                p.astype(jnp.bfloat16),
                held[b, TOKENS : 2 * TOKENS, :],
                NN,
                preferred_element_type=jnp.float32,
            )
            top[...] = jnp.broadcast_to(now, (TOKENS, WIDTH))

        o_ref[:, columns] = (mix[...] / total[...]).astype(jnp.bfloat16)


def attend(prior, has_own, has_before, last, whole_count, q_ref, own, *refs):
    refs = list(refs)
    take = lambda n: [refs.pop(0) for _ in range(n)]
    blocks = take(prior)
    before = take(2) if has_before else None
    whole = take(whole_count)
    outs = take(1 if last else 2)
    mixed, picked, causal, rows_in = take(4)
    head = pl.program_id(0)
    count = prior + has_own

    @pl.when(head == 0)
    def _():
        ids = ids_of(own)
        down = ids_down(ids)
        first = ids[0:1, 0:1]
        rows_in[...] = jnp.where(down == first, 1.0, 0.0)
        if has_own:
            down = jnp.concatenate([down, down], axis=1)
            row = lax.broadcasted_iota(jnp.int32, (TOKENS, TOKENS), 0)
            column = lax.broadcasted_iota(jnp.int32, (TOKENS, TOKENS), 1)
            same = down == ids_across(ids, TOKENS)
            causal[...] = jnp.where(same & (column <= row), 1.0, 0.0)
        for b in range(prior):
            picked[b] = ids_down(jnp.where(ids_of(blocks[b]) == first, 1.0, 0.0)).astype(
                jnp.bfloat16
            )

    for b in range(prior):
        mixed[b, :, 0:WIDTH] = blocks[b][TOKENS : 2 * TOKENS, :] * picked[b]
        mixed[b, :, WIDTH:] = picked[b]
    if has_own:
        mixed[prior, :, 0:WIDTH] = own[TOKENS : 2 * TOKENS, :]
        mixed[prior, :, WIDTH:] = jnp.ones((TOKENS, WIDTH), jnp.bfloat16)

    def term(q, keys, b, mask=None):
        s = lax.dot_general(q, keys, NT, preferred_element_type=jnp.float32)
        p = jnp.exp2(s * SCALE)
        if mask is not None:
            p = p * mask
        return lax.dot_general(
            p.astype(jnp.bfloat16), mixed[b], NN, preferred_element_type=jnp.float32
        )

    good = None
    weights = None
    lane = lax.broadcasted_iota(jnp.int32, (TOKENS, WIDTH), 1)
    for g in range(GROUP):
        columns = slice(g * WIDTH, (g + 1) * WIDTH)
        q = q_ref[:, columns]
        sums = term(q, blocks[0][0:TOKENS, :], 0)
        for b in range(1, prior):
            sums = sums + term(q, blocks[b][0:TOKENS, :], b)
        inside = rows_in[...] > 0.5
        mix = jnp.where(inside, sums[:, :WIDTH], 0.0)
        weight = jnp.where(inside, sums[:, WIDTH:], 0.0)
        if has_own:
            sums = term(q, own[0:TOKENS, :], prior, causal[...])
            mix = mix + sums[:, :WIDTH]
            weight = weight + sums[:, WIDTH:]
        if has_before:
            mix = mix + before[0][:, columns]
            weight = weight + before[1][:, g : g + 1]
        if last:
            outs[0][:, columns] = (mix / weight).astype(jnp.bfloat16)
            fine = jnp.where((weight > LOW) & (weight < HIGH), 1.0, 0.0)
            good = fine if good is None else jnp.minimum(good, fine)
        else:
            outs[0][:, columns] = mix
            weights = weight if weights is None else jnp.where(lane == g, weight, weights)
    if last:

        @pl.when(jnp.min(good) < 0.5)
        def _():
            general_head(head, whole, q_ref, outs[0], *refs)
    else:
        outs[1][...] = weights


def attention(queries, own, blocks, has_own, before, whole, last):
    by_head = lambda rows, columns: pl.BlockSpec((rows, columns), lambda h: (0, h))
    count = len(blocks) + has_own
    wide, narrow = by_head(TOKENS, GROUP * WIDTH), by_head(TOKENS, WIDTH)
    before_specs = [wide, narrow] if before else []
    if last:
        out_specs = wide
        out_shape = jax.ShapeDtypeStruct(queries.shape, jnp.bfloat16)
    else:
        out_specs = [wide, narrow]
        out_shape = [
            jax.ShapeDtypeStruct(queries.shape, jnp.float32),
            jax.ShapeDtypeStruct((TOKENS, KEY_VALUE_HEADS * WIDTH), jnp.float32),
        ]
    scratch = [
        pltpu.VMEM((count, TOKENS, 2 * WIDTH), jnp.bfloat16),
        pltpu.VMEM((len(blocks), TOKENS, WIDTH), jnp.bfloat16),
        pltpu.VMEM((TOKENS, TOKENS), jnp.float32),
        pltpu.VMEM((TOKENS, WIDTH), jnp.float32),
    ]
    if last:
        scratch += [
            pltpu.VMEM((len(whole), ROWS, WIDTH), jnp.bfloat16),
            pltpu.VMEM((TOKENS, WIDTH), jnp.float32),
            pltpu.VMEM((TOKENS, WIDTH), jnp.float32),
            pltpu.VMEM((TOKENS, WIDTH), jnp.float32),
            pltpu.SemaphoreType.DMA,
        ]
    return pl.pallas_call(
        functools.partial(attend, len(blocks), has_own, bool(before), last, len(whole)),
        grid=(KEY_VALUE_HEADS,),
        in_specs=[wide]
        + [by_head(ROWS, WIDTH)] * (1 + len(blocks))
        + before_specs
        + [pl.BlockSpec(memory_space=pl.ANY)] * len(whole),
        out_specs=out_specs,
        out_shape=out_shape,
        scratch_shapes=scratch,
        compiler_params=pltpu.CompilerParams(vmem_limit_bytes=VMEM_LIMIT),
        cost_estimate=pl.CostEstimate(
            flops=28 * 256 * 256 * count * 1024,
            bytes_accessed=4_000_000 + count * 540_000,
            transcendentals=28 * 256 * 256 * count,
        ),
    )(queries, own, *blocks, *before, *whole)


def per_device(queries, key_states, value_vectors, segment_ids):
    ids = (segment_ids + 1).astype(jnp.bfloat16).reshape(2, WIDTH)
    ids = jnp.pad(jnp.tile(ids, (1, KEY_VALUE_HEADS)), ((0, EXTRA - 2), (0, 0)))
    own = jnp.concatenate([key_states, value_vectors, ids], axis=0)
    x = lax.axis_index("seq") % 4
    four = row_on(own)
    back = turned_along_y(own, -1)
    across = turned_along_x(own, 2)
    middle = [turned_along_x(four, a) for a in (1, 3)]
    eight = two_rows_on(back)
    next_across = row_on(across)
    ends = [turned_along_x(jnp.where(x + a < 4, own, eight), a) for a in (1, 3)]
    far_across = row_on(next_across, (0, 1))
    across = jnp.where(x < 2, far_across, across)
    early = [four, *middle, next_across, eight]
    late = [*ends, across]
    stage = attention(queries, own, early, True, [], [], False)
    return attention(queries, own, late, False, stage, [*early, *late, own], True)


def solution(mesh):
    rows = P(AXES, None)
    return jax.shard_map(
        per_device,
        mesh=mesh,
        in_specs=(rows, rows, rows, P(AXES)),
        out_specs=rows,
        check_vma=False,
    )
```

```python
import functools

import jax
import jax.numpy as jnp
from jax import lax
from jax.experimental import pallas as pl
from jax.experimental.pallas import tpu as pltpu
from jax.sharding import PartitionSpec as P

KEY_VALUE_HEADS = 4
GROUP = 7
WIDTH = 128
TOKENS = 256
EXTRA = 16
ROWS = 2 * TOKENS + EXTRA
AXES = ("dp", "seq")
SCALE = 1.4426950408889634 / WIDTH**0.5
LOW, HIGH = 1e-25, 1e30
VMEM_LIMIT = 24 * 1024 * 1024
NT = (((1,), (1,)), ((), ()))
NN = (((1,), (0,)), ((), ()))


def rank_of(plane, y, x):
    return (plane * 4 + y) * 4 + x


def turned_along_x(value, steps):
    pairs = [
        (rank_of(plane, y, x), rank_of(plane, y, (x + steps) % 4))
        for plane in range(16)
        for y in range(4)
        for x in range(4)
    ]
    return lax.ppermute(value, AXES, pairs)


def turned_along_y(value, steps):
    pairs = [
        (rank_of(plane, y, x), rank_of(plane, (y + steps) % 4, x))
        for plane in range(16)
        for y in range(4)
        for x in range(4)
    ]
    return lax.ppermute(value, AXES, pairs)


def two_rows_on(value):
    pairs = [
        (rank_of(plane, (y - 1) % 4, x), (rank_of(plane, y, x) + 8) % 256)
        for plane in range(16)
        for y in range(4)
        for x in range(4)
    ]
    return lax.ppermute(value, AXES, pairs)


def row_on(value):
    return lax.ppermute(value, AXES, [(r, (r + 4) % 256) for r in range(256)])


def ids_down(rows):
    halves = [
        jnp.transpose(jnp.broadcast_to(rows[i : i + 1], (WIDTH, WIDTH))) for i in range(2)
    ]
    return jnp.concatenate(halves, axis=0)


def ids_across(rows, count):
    halves = [jnp.broadcast_to(rows[i : i + 1], (count, WIDTH)) for i in range(2)]
    return jnp.concatenate(halves, axis=1)


def ids_of(block):
    return block[2 * TOKENS : ROWS, :].astype(jnp.float32)[0:2]


def general_head(head, whole, q_ref, o_ref, held, top, total, mix, sem):
    count = len(whole)
    for b in range(count):
        columns = pl.ds(pl.multiple_of(head * WIDTH, WIDTH), WIDTH)
        copy = pltpu.make_async_copy(whole[b].at[:, columns], held.at[b], sem)
        copy.start()
        copy.wait()
    mine = ids_down(ids_of(held[count - 1]))
    mine = jnp.concatenate([mine, mine], axis=1)
    later = lax.broadcasted_iota(jnp.int32, (TOKENS, TOKENS), 1) > lax.broadcasted_iota(
        jnp.int32, (TOKENS, TOKENS), 0
    )

    @pl.loop(0, GROUP)
    def _(g):
        columns = pl.ds(pl.multiple_of(g * WIDTH, WIDTH), WIDTH)
        top[...] = jnp.full((TOKENS, WIDTH), -1e30, jnp.float32)
        total[...] = jnp.zeros((TOKENS, WIDTH), jnp.float32)
        mix[...] = jnp.zeros((TOKENS, WIDTH), jnp.float32)

        @pl.loop(0, count)
        def _(b):
            s = lax.dot_general(
                q_ref[:, columns], held[b, 0:TOKENS, :], NT, preferred_element_type=jnp.float32
            )
            s = s * SCALE
            theirs = ids_across(
                held[b, 2 * TOKENS : ROWS, :].astype(jnp.float32)[0:2], TOKENS
            )
            allowed = (mine == theirs) & ~(later & (b == count - 1))
            s = jnp.where(allowed, s, -1e30)
            now = jnp.maximum(top[:, 0:1], jnp.max(s, axis=1, keepdims=True))
            p = jnp.where(allowed, jnp.exp2(s - now), 0.0)
            keep = jnp.exp2(top[:, 0:1] - now)
            total[...] = total[...] * keep + jnp.sum(p, axis=1, keepdims=True)
            mix[...] = mix[...] * keep + lax.dot_general(
                p.astype(jnp.bfloat16),
                held[b, TOKENS : 2 * TOKENS, :],
                NN,
                preferred_element_type=jnp.float32,
            )
            top[...] = jnp.broadcast_to(now, (TOKENS, WIDTH))

        o_ref[:, columns] = (mix[...] / total[...]).astype(jnp.bfloat16)


def attend(prior, has_own, has_before, last, whole_count, q_ref, own, *refs):
    refs = list(refs)
    take = lambda n: [refs.pop(0) for _ in range(n)]
    blocks = take(prior)
    before = take(2) if has_before else None
    whole = take(whole_count)
    outs = take(1 if last else 2)
    mixed, picked, causal, rows_in = take(4)
    head = pl.program_id(0)
    count = prior + has_own

    @pl.when(head == 0)
    def _():
        ids = ids_of(own)
        down = ids_down(ids)
        first = ids[0:1, 0:1]
        rows_in[...] = jnp.where(down == first, 1.0, 0.0)
        if has_own:
            down = jnp.concatenate([down, down], axis=1)
            row = lax.broadcasted_iota(jnp.int32, (TOKENS, TOKENS), 0)
            column = lax.broadcasted_iota(jnp.int32, (TOKENS, TOKENS), 1)
            same = down == ids_across(ids, TOKENS)
            causal[...] = jnp.where(same & (column <= row), 1.0, 0.0)
        for b in range(prior):
            picked[b] = ids_down(jnp.where(ids_of(blocks[b]) == first, 1.0, 0.0)).astype(
                jnp.bfloat16
            )

    for b in range(prior):
        mixed[b, :, 0:WIDTH] = blocks[b][TOKENS : 2 * TOKENS, :] * picked[b]
        mixed[b, :, WIDTH:] = picked[b]
    if has_own:
        mixed[prior, :, 0:WIDTH] = own[TOKENS : 2 * TOKENS, :]
        mixed[prior, :, WIDTH:] = jnp.ones((TOKENS, WIDTH), jnp.bfloat16)

    def term(q, keys, b, mask=None):
        s = lax.dot_general(q, keys, NT, preferred_element_type=jnp.float32)
        p = jnp.exp2(s * SCALE)
        if mask is not None:
            p = p * mask
        return lax.dot_general(
            p.astype(jnp.bfloat16), mixed[b], NN, preferred_element_type=jnp.float32
        )

    good = None
    weights = None
    lane = lax.broadcasted_iota(jnp.int32, (TOKENS, WIDTH), 1)
    for g in range(GROUP):
        columns = slice(g * WIDTH, (g + 1) * WIDTH)
        q = q_ref[:, columns]
        mix, weight = 0.0, 0.0
        if prior:
            sums = term(q, blocks[0][0:TOKENS, :], 0)
            for b in range(1, prior):
                sums = sums + term(q, blocks[b][0:TOKENS, :], b)
            inside = rows_in[...] > 0.5
            mix = jnp.where(inside, sums[:, :WIDTH], 0.0)
            weight = jnp.where(inside, sums[:, WIDTH:], 0.0)
        if has_own:
            sums = term(q, own[0:TOKENS, :], prior, causal[...])
            mix = mix + sums[:, :WIDTH]
            weight = weight + sums[:, WIDTH:]
        if has_before:
            mix = mix + before[0][:, columns]
            weight = weight + before[1][:, g : g + 1]
        if last:
            outs[0][:, columns] = (mix / weight).astype(jnp.bfloat16)
            fine = jnp.where((weight > LOW) & (weight < HIGH), 1.0, 0.0)
            good = fine if good is None else jnp.minimum(good, fine)
        else:
            outs[0][:, columns] = mix
            weights = weight if weights is None else jnp.where(lane == g, weight, weights)
    if last:

        @pl.when(jnp.min(good) < 0.5)
        def _():
            general_head(head, whole, q_ref, outs[0], *refs)
    else:
        outs[1][...] = weights


def attention(queries, own, blocks, has_own, before, whole, last):
    by_head = lambda rows, columns: pl.BlockSpec((rows, columns), lambda h: (0, h))
    count = len(blocks) + has_own
    wide, narrow = by_head(TOKENS, GROUP * WIDTH), by_head(TOKENS, WIDTH)
    before_specs = [wide, narrow] if before else []
    if last:
        out_specs = wide
        out_shape = jax.ShapeDtypeStruct(queries.shape, jnp.bfloat16)
    else:
        out_specs = [wide, narrow]
        out_shape = [
            jax.ShapeDtypeStruct(queries.shape, jnp.float32),
            jax.ShapeDtypeStruct((TOKENS, KEY_VALUE_HEADS * WIDTH), jnp.float32),
        ]
    scratch = [
        pltpu.VMEM((count, TOKENS, 2 * WIDTH), jnp.bfloat16),
        pltpu.VMEM((max(len(blocks), 1), TOKENS, WIDTH), jnp.bfloat16),
        pltpu.VMEM((TOKENS, TOKENS), jnp.float32),
        pltpu.VMEM((TOKENS, WIDTH), jnp.float32),
    ]
    if last:
        scratch += [
            pltpu.VMEM((len(whole), ROWS, WIDTH), jnp.bfloat16),
            pltpu.VMEM((TOKENS, WIDTH), jnp.float32),
            pltpu.VMEM((TOKENS, WIDTH), jnp.float32),
            pltpu.VMEM((TOKENS, WIDTH), jnp.float32),
            pltpu.SemaphoreType.DMA,
        ]
    return pl.pallas_call(
        functools.partial(attend, len(blocks), has_own, bool(before), last, len(whole)),
        grid=(KEY_VALUE_HEADS,),
        in_specs=[wide]
        + [by_head(ROWS, WIDTH)] * (1 + len(blocks))
        + before_specs
        + [pl.BlockSpec(memory_space=pl.ANY)] * len(whole),
        out_specs=out_specs,
        out_shape=out_shape,
        scratch_shapes=scratch,
        compiler_params=pltpu.CompilerParams(vmem_limit_bytes=VMEM_LIMIT),
        cost_estimate=pl.CostEstimate(
            flops=28 * 256 * 256 * count * 1024,
            bytes_accessed=4_000_000 + count * 540_000,
            transcendentals=28 * 256 * 256 * count,
        ),
    )(queries, own, *blocks, *before, *whole)


def per_device(queries, key_states, value_vectors, segment_ids):
    ids = (segment_ids + 1).astype(jnp.bfloat16).reshape(2, WIDTH)
    ids = jnp.pad(jnp.tile(ids, (1, KEY_VALUE_HEADS)), ((0, EXTRA - 2), (0, 0)))
    own = jnp.concatenate([key_states, value_vectors, ids], axis=0)
    x = lax.axis_index("seq") % 4
    own = lax.optimization_barrier(own)
    four = row_on(own)
    back = turned_along_y(own, -1)
    across = turned_along_x(own, 2)
    stage = attention(queries, own, [], True, [], [], False)
    four, back, across, *stage = lax.optimization_barrier((four, back, across, *stage))
    middle = [turned_along_x(four, a) for a in (1, 3)]
    eight = two_rows_on(back)
    next_across = row_on(across)
    ends = [turned_along_x(jnp.where(x + a < 4, own, eight), a) for a in (1, 3)]
    far_across = row_on(next_across)
    across = jnp.where(x < 2, far_across, across)
    early = [four, *middle, next_across, eight]
    late = [*ends, across]
    stage = attention(queries, own, early, False, stage, [], False)
    return attention(queries, own, late, False, stage, [*early, *late, own], True)


def solution(mesh):
    rows = P(AXES, None)
    return jax.shard_map(
        per_device,
        mesh=mesh,
        in_specs=(rows, rows, rows, P(AXES)),
        out_specs=rows,
        check_vma=False,
    )
```

```python
import functools

import jax
import jax.numpy as jnp
from jax import lax
from jax.experimental import pallas as pl
from jax.experimental.pallas import tpu as pltpu
from jax.sharding import PartitionSpec as P

KEY_VALUE_HEADS = 4
GROUP = 7
WIDTH = 128
TOKENS = 256
EXTRA = 16
ROWS = 2 * TOKENS + EXTRA
AXES = ("dp", "seq")
SCALE = 1.4426950408889634 / WIDTH**0.5
LOW, HIGH = 1e-25, 1e30
VMEM_LIMIT = 16 * 1024 * 1024
NT = (((1,), (1,)), ((), ()))
NN = (((1,), (0,)), ((), ()))


def rank_of(plane, y, x):
    return (plane * 4 + y) * 4 + x


def turned_along_x(value, steps):
    pairs = [
        (rank_of(plane, y, x), rank_of(plane, y, (x + steps) % 4))
        for plane in range(16)
        for y in range(4)
        for x in range(4)
    ]
    return lax.ppermute(value, AXES, pairs)


def turned_along_y(value, steps):
    pairs = [
        (rank_of(plane, y, x), rank_of(plane, (y + steps) % 4, x))
        for plane in range(16)
        for y in range(4)
        for x in range(4)
    ]
    return lax.ppermute(value, AXES, pairs)


def two_rows_on(value):
    pairs = [
        (rank_of(plane, (y - 1) % 4, x), (rank_of(plane, y, x) + 8) % 256)
        for plane in range(16)
        for y in range(4)
        for x in range(4)
    ]
    return lax.ppermute(value, AXES, pairs)


def row_on(value):
    return lax.ppermute(value, AXES, [(r, (r + 4) % 256) for r in range(256)])


def ids_down(rows):
    halves = [
        jnp.transpose(jnp.broadcast_to(rows[i : i + 1], (WIDTH, WIDTH))) for i in range(2)
    ]
    return jnp.concatenate(halves, axis=0)


def ids_across(rows, count):
    halves = [jnp.broadcast_to(rows[i : i + 1], (count, WIDTH)) for i in range(2)]
    return jnp.concatenate(halves, axis=1)


def ids_of(block):
    return block[2 * TOKENS : ROWS, :].astype(jnp.float32)[0:2]


def general_head(head, whole, q_ref, o_ref, held, top, total, mix, sem):
    count = len(whole)
    for b in range(count):
        columns = pl.ds(pl.multiple_of(head * WIDTH, WIDTH), WIDTH)
        copy = pltpu.make_async_copy(whole[b].at[:, columns], held.at[b], sem)
        copy.start()
        copy.wait()
    mine = ids_down(ids_of(held[count - 1]))
    mine = jnp.concatenate([mine, mine], axis=1)
    later = lax.broadcasted_iota(jnp.int32, (TOKENS, TOKENS), 1) > lax.broadcasted_iota(
        jnp.int32, (TOKENS, TOKENS), 0
    )

    @pl.loop(0, GROUP)
    def _(g):
        columns = pl.ds(pl.multiple_of(g * WIDTH, WIDTH), WIDTH)
        top[...] = jnp.full((TOKENS, WIDTH), -1e30, jnp.float32)
        total[...] = jnp.zeros((TOKENS, WIDTH), jnp.float32)
        mix[...] = jnp.zeros((TOKENS, WIDTH), jnp.float32)

        @pl.loop(0, count)
        def _(b):
            s = lax.dot_general(
                q_ref[:, columns], held[b, 0:TOKENS, :], NT, preferred_element_type=jnp.float32
            )
            s = s * SCALE
            theirs = ids_across(
                held[b, 2 * TOKENS : ROWS, :].astype(jnp.float32)[0:2], TOKENS
            )
            allowed = (mine == theirs) & ~(later & (b == count - 1))
            s = jnp.where(allowed, s, -1e30)
            now = jnp.maximum(top[:, 0:1], jnp.max(s, axis=1, keepdims=True))
            p = jnp.where(allowed, jnp.exp2(s - now), 0.0)
            keep = jnp.exp2(top[:, 0:1] - now)
            total[...] = total[...] * keep + jnp.sum(p, axis=1, keepdims=True)
            mix[...] = mix[...] * keep + lax.dot_general(
                p.astype(jnp.bfloat16),
                held[b, TOKENS : 2 * TOKENS, :],
                NN,
                preferred_element_type=jnp.float32,
            )
            top[...] = jnp.broadcast_to(now, (TOKENS, WIDTH))

        o_ref[:, columns] = (mix[...] / total[...]).astype(jnp.bfloat16)


def attend(prior, has_own, has_before, last, whole_count, q_ref, own, *refs):
    refs = list(refs)
    take = lambda n: [refs.pop(0) for _ in range(n)]
    blocks = take(prior)
    before = take(2) if has_before else None
    whole = take(whole_count)
    outs = take(1 if last else 3)
    mixed, picked, causal, rows_in = take(4)
    head = pl.program_id(0)
    count = prior + has_own

    @pl.when(head == 0)
    def _():
        ids = ids_of(own)
        down = ids_down(ids)
        first = ids[0:1, 0:1]
        rows_in[...] = jnp.where(down == first, 1.0, 0.0)
        if has_own:
            down = jnp.concatenate([down, down], axis=1)
            row = lax.broadcasted_iota(jnp.int32, (TOKENS, TOKENS), 0)
            column = lax.broadcasted_iota(jnp.int32, (TOKENS, TOKENS), 1)
            same = down == ids_across(ids, TOKENS)
            causal[...] = jnp.where(same & (column <= row), 1.0, 0.0)
        for b in range(prior):
            picked[b] = ids_down(jnp.where(ids_of(blocks[b]) == first, 1.0, 0.0)).astype(
                jnp.bfloat16
            )

    for b in range(prior):
        mixed[b, :, 0:WIDTH] = blocks[b][TOKENS : 2 * TOKENS, :] * picked[b]
        mixed[b, :, WIDTH:] = picked[b]
    if has_own:
        mixed[prior, :, 0:WIDTH] = own[TOKENS : 2 * TOKENS, :]
        mixed[prior, :, WIDTH:] = jnp.ones((TOKENS, WIDTH), jnp.bfloat16)

    def term(q, keys, b, mask=None):
        s = lax.dot_general(q, keys, NT, preferred_element_type=jnp.float32)
        p = jnp.exp2(s * SCALE)
        if mask is not None:
            p = p * mask
        return lax.dot_general(
            p.astype(jnp.bfloat16), mixed[b], NN, preferred_element_type=jnp.float32
        )

    good = None
    weights = None
    lane = lax.broadcasted_iota(jnp.int32, (TOKENS, WIDTH), 1)
    for g in range(GROUP):
        columns = slice(g * WIDTH, (g + 1) * WIDTH)
        q = q_ref[:, columns]
        mix, weight = 0.0, 0.0
        if prior:
            sums = term(q, blocks[0][0:TOKENS, :], 0)
            for b in range(1, prior):
                sums = sums + term(q, blocks[b][0:TOKENS, :], b)
            inside = rows_in[...] > 0.5
            mix = jnp.where(inside, sums[:, :WIDTH], 0.0)
            weight = jnp.where(inside, sums[:, WIDTH:], 0.0)
        if has_own:
            sums = term(q, own[0:TOKENS, :], prior, causal[...])
            mix = mix + sums[:, :WIDTH]
            weight = weight + sums[:, WIDTH:]
        if has_before:
            mix = mix + before[0][:, columns]
            weight = weight + before[1][:, g : g + 1]
        if last:
            outs[0][:, columns] = (mix / weight).astype(jnp.bfloat16)
            fine = jnp.where((weight > LOW) & (weight < HIGH), 1.0, 0.0)
            good = fine if good is None else jnp.minimum(good, fine)
        else:
            outs[0][:, columns] = mix
            weights = weight if weights is None else jnp.where(lane == g, weight, weights)
    if last:

        @pl.when(jnp.min(good) < 0.5)
        def _():
            general_head(head, whole, q_ref, outs[0], *refs)
    else:
        outs[1][...] = weights
        outs[2][...] = jnp.zeros_like(outs[2])


def attention(queries, own, blocks, has_own, before, whole, last):
    by_head = lambda rows, columns: pl.BlockSpec((rows, columns), lambda h: (0, h))
    count = len(blocks) + has_own
    wide, narrow = by_head(TOKENS, GROUP * WIDTH), by_head(TOKENS, WIDTH)
    before_specs = [wide, narrow] if before else []
    if last:
        out_specs = wide
        out_shape = jax.ShapeDtypeStruct(queries.shape, jnp.bfloat16)
    else:
        out_specs = [wide, narrow, by_head(8, WIDTH)]
        out_shape = [
            jax.ShapeDtypeStruct(queries.shape, jnp.float32),
            jax.ShapeDtypeStruct((TOKENS, KEY_VALUE_HEADS * WIDTH), jnp.float32),
            jax.ShapeDtypeStruct((8, KEY_VALUE_HEADS * WIDTH), jnp.float32),
        ]
    scratch = [
        pltpu.VMEM((count, TOKENS, 2 * WIDTH), jnp.bfloat16),
        pltpu.VMEM((max(len(blocks), 1), TOKENS, WIDTH), jnp.bfloat16),
        pltpu.VMEM((TOKENS, TOKENS), jnp.float32),
        pltpu.VMEM((TOKENS, WIDTH), jnp.float32),
    ]
    if last:
        scratch += [
            pltpu.VMEM((len(whole), ROWS, WIDTH), jnp.bfloat16),
            pltpu.VMEM((TOKENS, WIDTH), jnp.float32),
            pltpu.VMEM((TOKENS, WIDTH), jnp.float32),
            pltpu.VMEM((TOKENS, WIDTH), jnp.float32),
            pltpu.SemaphoreType.DMA,
        ]
    return pl.pallas_call(
        functools.partial(attend, len(blocks), has_own, bool(before), last, len(whole)),
        grid=(KEY_VALUE_HEADS,),
        in_specs=[wide]
        + [by_head(ROWS, WIDTH)] * (1 + len(blocks))
        + before_specs
        + [pl.BlockSpec(memory_space=pl.ANY)] * len(whole),
        out_specs=out_specs,
        out_shape=out_shape,
        scratch_shapes=scratch,
        compiler_params=pltpu.CompilerParams(vmem_limit_bytes=VMEM_LIMIT),
        cost_estimate=pl.CostEstimate(
            flops=28 * 256 * 256 * count * 1024,
            bytes_accessed=4_000_000 + count * 540_000,
            transcendentals=28 * 256 * 256 * count,
        ),
    )(queries, own, *blocks, *before, *whole)


def per_device(queries, key_states, value_vectors, segment_ids):
    ids = (segment_ids + 1).astype(jnp.bfloat16).reshape(2, WIDTH)
    ids = jnp.pad(jnp.tile(ids, (1, KEY_VALUE_HEADS)), ((0, EXTRA - 2), (0, 0)))
    own = jnp.concatenate([key_states, value_vectors, ids], axis=0)
    x = lax.axis_index("seq") % 4
    own = lax.optimization_barrier(own)
    four = row_on(own)
    back = turned_along_y(own, -1)
    across = turned_along_x(own, 2)
    middle = [turned_along_x(four, a) for a in (1, 3)]
    eight = two_rows_on(back)
    next_across = row_on(across)
    *stage, done = attention(queries, own, [four], True, [], [], False)
    eight, _ = lax.optimization_barrier((eight, done))
    ends = [turned_along_x(jnp.where(x + a < 4, own, eight), a) for a in (1, 3)]
    far_across = row_on(next_across)
    across = jnp.where(x < 2, far_across, across)
    early = [*middle, next_across, eight]
    late = [*ends, across]
    *stage, _ = attention(queries, own, early, False, stage, [], False)
    return attention(queries, own, late, False, stage, [four, *early, *late, own], True)


def solution(mesh):
    rows = P(AXES, None)
    return jax.shard_map(
        per_device,
        mesh=mesh,
        in_specs=(rows, rows, rows, P(AXES)),
        out_specs=rows,
        check_vma=False,
    )
```

```python
import functools

import jax
import jax.numpy as jnp
from jax import lax
from jax.experimental import pallas as pl
from jax.experimental.pallas import tpu as pltpu
from jax.sharding import PartitionSpec as P

KEY_VALUE_HEADS = 4
GROUP = 7
WIDTH = 128
TOKENS = 256
EXTRA = 16
ROWS = 2 * TOKENS + EXTRA
AXES = ("dp", "seq")
SCALE = 1.4426950408889634 / WIDTH**0.5
LOW, HIGH = 1e-25, 1e30
VMEM_LIMIT = 16 * 1024 * 1024
NT = (((1,), (1,)), ((), ()))
NN = (((1,), (0,)), ((), ()))


def rank_of(plane, y, x):
    return (plane * 4 + y) * 4 + x


def turned_along_x(value, steps):
    pairs = [
        (rank_of(plane, y, x), rank_of(plane, y, (x + steps) % 4))
        for plane in range(16)
        for y in range(4)
        for x in range(4)
    ]
    return lax.ppermute(value, AXES, pairs)


def turned_along_y(value, steps):
    pairs = [
        (rank_of(plane, y, x), rank_of(plane, (y + steps) % 4, x))
        for plane in range(16)
        for y in range(4)
        for x in range(4)
    ]
    return lax.ppermute(value, AXES, pairs)


def two_rows_on(value):
    pairs = [
        (rank_of(plane, (y - 1) % 4, x), (rank_of(plane, y, x) + 8) % 256)
        for plane in range(16)
        for y in range(4)
        for x in range(4)
    ]
    return lax.ppermute(value, AXES, pairs)


def rows_on(value, rows):
    return lax.ppermute(value, AXES, [(r, (r + 4 * rows) % 256) for r in range(256)])


def ids_down(rows):
    halves = [
        jnp.transpose(jnp.broadcast_to(rows[i : i + 1], (WIDTH, WIDTH))) for i in range(2)
    ]
    return jnp.concatenate(halves, axis=0)


def ids_across(rows, count):
    halves = [jnp.broadcast_to(rows[i : i + 1], (count, WIDTH)) for i in range(2)]
    return jnp.concatenate(halves, axis=1)


def ids_of(block):
    return block[2 * TOKENS : ROWS, :].astype(jnp.float32)[0:2]


def general_head(head, whole, chosen, q_ref, o_ref, held, top, total, mix, sem):
    count = len(whole) + 1
    held[count - 2] = chosen[...]
    for b, place in enumerate([*range(count - 2), count - 1]):
        columns = pl.ds(pl.multiple_of(head * WIDTH, WIDTH), WIDTH)
        copy = pltpu.make_async_copy(whole[b].at[:, columns], held.at[place], sem)
        copy.start()
        copy.wait()
    mine = ids_down(ids_of(held[count - 1]))
    mine = jnp.concatenate([mine, mine], axis=1)
    later = lax.broadcasted_iota(jnp.int32, (TOKENS, TOKENS), 1) > lax.broadcasted_iota(
        jnp.int32, (TOKENS, TOKENS), 0
    )

    @pl.loop(0, GROUP)
    def _(g):
        columns = pl.ds(pl.multiple_of(g * WIDTH, WIDTH), WIDTH)
        top[...] = jnp.full((TOKENS, WIDTH), -1e30, jnp.float32)
        total[...] = jnp.zeros((TOKENS, WIDTH), jnp.float32)
        mix[...] = jnp.zeros((TOKENS, WIDTH), jnp.float32)

        @pl.loop(0, count)
        def _(b):
            s = lax.dot_general(
                q_ref[:, columns], held[b, 0:TOKENS, :], NT, preferred_element_type=jnp.float32
            )
            s = s * SCALE
            theirs = ids_across(
                held[b, 2 * TOKENS : ROWS, :].astype(jnp.float32)[0:2], TOKENS
            )
            allowed = (mine == theirs) & ~(later & (b == count - 1))
            s = jnp.where(allowed, s, -1e30)
            now = jnp.maximum(top[:, 0:1], jnp.max(s, axis=1, keepdims=True))
            p = jnp.where(allowed, jnp.exp2(s - now), 0.0)
            keep = jnp.exp2(top[:, 0:1] - now)
            total[...] = total[...] * keep + jnp.sum(p, axis=1, keepdims=True)
            mix[...] = mix[...] * keep + lax.dot_general(
                p.astype(jnp.bfloat16),
                held[b, TOKENS : 2 * TOKENS, :],
                NN,
                preferred_element_type=jnp.float32,
            )
            top[...] = jnp.broadcast_to(now, (TOKENS, WIDTH))

        o_ref[:, columns] = (mix[...] / total[...]).astype(jnp.bfloat16)


def attend(prior, has_own, has_before, last, whole_count, *refs):
    refs = list(refs)
    take = lambda n: [refs.pop(0) for _ in range(n)]
    which = take(1)[0] if last else None
    q_ref, own = take(2)
    blocks = take(prior)
    before = take(2) if has_before else None
    whole = take(whole_count)
    outs = take(1 if last else 3)
    mixed, picked, causal, rows_in = take(4)
    head = pl.program_id(0)
    if last:
        chosen = take(1)[0]
        latter = blocks.pop()
        chosen[...] = jnp.where(which[0] == 1, latter[...], blocks[-1][...])
        blocks[-1] = chosen
        prior -= 1

    @pl.when(head == 0)
    def _():
        ids = ids_of(own)
        down = ids_down(ids)
        first = ids[0:1, 0:1]
        rows_in[...] = jnp.where(down == first, 1.0, 0.0)
        if has_own:
            down = jnp.concatenate([down, down], axis=1)
            row = lax.broadcasted_iota(jnp.int32, (TOKENS, TOKENS), 0)
            column = lax.broadcasted_iota(jnp.int32, (TOKENS, TOKENS), 1)
            same = down == ids_across(ids, TOKENS)
            causal[...] = jnp.where(same & (column <= row), 1.0, 0.0)
        for b in range(prior):
            picked[b] = ids_down(jnp.where(ids_of(blocks[b]) == first, 1.0, 0.0)).astype(
                jnp.bfloat16
            )

    for b in range(prior):
        mixed[b, :, 0:WIDTH] = blocks[b][TOKENS : 2 * TOKENS, :] * picked[b]
        mixed[b, :, WIDTH:] = picked[b]
    if has_own:
        mixed[prior, :, 0:WIDTH] = own[TOKENS : 2 * TOKENS, :]
        mixed[prior, :, WIDTH:] = jnp.ones((TOKENS, WIDTH), jnp.bfloat16)

    def term(q, keys, b, mask=None):
        s = lax.dot_general(q, keys, NT, preferred_element_type=jnp.float32)
        p = jnp.exp2(s * SCALE)
        if mask is not None:
            p = p * mask
        return lax.dot_general(
            p.astype(jnp.bfloat16), mixed[b], NN, preferred_element_type=jnp.float32
        )

    good = None
    weights = None
    lane = lax.broadcasted_iota(jnp.int32, (TOKENS, WIDTH), 1)
    for g in range(GROUP):
        columns = slice(g * WIDTH, (g + 1) * WIDTH)
        q = q_ref[:, columns]
        mix, weight = 0.0, 0.0
        if prior:
            sums = term(q, blocks[0][0:TOKENS, :], 0)
            for b in range(1, prior):
                sums = sums + term(q, blocks[b][0:TOKENS, :], b)
            inside = rows_in[...] > 0.5
            mix = jnp.where(inside, sums[:, :WIDTH], 0.0)
            weight = jnp.where(inside, sums[:, WIDTH:], 0.0)
        if has_own:
            sums = term(q, own[0:TOKENS, :], prior, causal[...])
            mix = mix + sums[:, :WIDTH]
            weight = weight + sums[:, WIDTH:]
        if has_before:
            mix = mix + before[0][:, columns]
            weight = weight + before[1][:, g : g + 1]
        if last:
            outs[0][:, columns] = (mix / weight).astype(jnp.bfloat16)
            fine = jnp.where((weight > LOW) & (weight < HIGH), 1.0, 0.0)
            good = fine if good is None else jnp.minimum(good, fine)
        else:
            outs[0][:, columns] = mix
            weights = weight if weights is None else jnp.where(lane == g, weight, weights)
    if last:

        @pl.when(jnp.min(good) < 0.5)
        def _():
            general_head(head, whole, chosen, q_ref, outs[0], *refs)
    else:
        outs[1][...] = weights
        outs[2][...] = jnp.zeros_like(outs[2])


def attention(queries, own, blocks, has_own, before, whole, which):
    by_head = lambda rows, columns: pl.BlockSpec((rows, columns), lambda h: (0, h))
    last = which is not None
    count = len(blocks) + has_own - last
    wide, narrow = by_head(TOKENS, GROUP * WIDTH), by_head(TOKENS, WIDTH)
    before_specs = [wide, narrow] if before else []
    if last:
        out_specs = wide
        out_shape = jax.ShapeDtypeStruct(queries.shape, jnp.bfloat16)
    else:
        out_specs = [wide, narrow, by_head(8, WIDTH)]
        out_shape = [
            jax.ShapeDtypeStruct(queries.shape, jnp.float32),
            jax.ShapeDtypeStruct((TOKENS, KEY_VALUE_HEADS * WIDTH), jnp.float32),
            jax.ShapeDtypeStruct((8, KEY_VALUE_HEADS * WIDTH), jnp.float32),
        ]
    scratch = [
        pltpu.VMEM((count, TOKENS, 2 * WIDTH), jnp.bfloat16),
        pltpu.VMEM((max(len(blocks), 1), TOKENS, WIDTH), jnp.bfloat16),
        pltpu.VMEM((TOKENS, TOKENS), jnp.float32),
        pltpu.VMEM((TOKENS, WIDTH), jnp.float32),
    ]
    if last:
        scratch += [
            pltpu.VMEM((ROWS, WIDTH), jnp.bfloat16),
            pltpu.VMEM((len(whole) + 1, ROWS, WIDTH), jnp.bfloat16),
            pltpu.VMEM((TOKENS, WIDTH), jnp.float32),
            pltpu.VMEM((TOKENS, WIDTH), jnp.float32),
            pltpu.VMEM((TOKENS, WIDTH), jnp.float32),
            pltpu.SemaphoreType.DMA,
        ]
    return pl.pallas_call(
        functools.partial(attend, len(blocks), has_own, bool(before), last, len(whole)),
        grid=(KEY_VALUE_HEADS,),
        in_specs=[pl.BlockSpec(memory_space=pltpu.SMEM)] * last
        + [wide]
        + [by_head(ROWS, WIDTH)] * (1 + len(blocks))
        + before_specs
        + [pl.BlockSpec(memory_space=pl.ANY)] * len(whole),
        out_specs=out_specs,
        out_shape=out_shape,
        scratch_shapes=scratch,
        compiler_params=pltpu.CompilerParams(vmem_limit_bytes=VMEM_LIMIT),
        cost_estimate=pl.CostEstimate(
            flops=28 * 256 * 256 * count * 1024,
            bytes_accessed=4_000_000 + count * 540_000,
            transcendentals=28 * 256 * 256 * count,
        ),
    )(*([which.astype(jnp.int32)] if last else []), queries, own, *blocks, *before, *whole)


def per_device(queries, key_states, value_vectors, segment_ids):
    ids = segment_ids.astype(jnp.bfloat16).reshape(2, WIDTH)
    ids = jnp.pad(jnp.tile(ids, (1, KEY_VALUE_HEADS)), ((0, EXTRA - 2), (0, 0)))
    own = jnp.concatenate([key_states, value_vectors, ids], axis=0)
    x = lax.axis_index("seq") % 4
    own = lax.optimization_barrier(own)
    four = rows_on(own, 1)
    back = turned_along_y(own, -1)
    across = turned_along_x(own, 2)
    middle = [turned_along_x(four, a) for a in (1, 3)]
    eight = two_rows_on(back)
    next_across = rows_on(across, 1)
    *stage, done = attention(queries, own, [four], True, [], [], None)
    eight, _ = lax.optimization_barrier((eight, done))
    ends = [turned_along_x(jnp.where(x + a < 4, own, eight), a) for a in (1, 3)]
    across, next_across = lax.optimization_barrier((across, next_across))
    far_across = rows_on(across, 2)
    early = [*middle, next_across, eight]
    *stage, _ = attention(queries, own, early, False, stage, [], None)
    late = [*ends, across, far_across]
    whole = [four, *early, *ends, own]
    return attention(queries, own, late, False, stage, whole, jnp.reshape(x < 2, (1,)))


def solution(mesh):
    rows = P(AXES, None)
    return jax.shard_map(
        per_device,
        mesh=mesh,
        in_specs=(rows, rows, rows, P(AXES)),
        out_specs=rows,
        check_vma=False,
    )
```

```python
import functools

import jax
import jax.numpy as jnp
from jax import lax
from jax.experimental import pallas as pl
from jax.experimental.pallas import tpu as pltpu
from jax.sharding import PartitionSpec as P

KEY_VALUE_HEADS = 4
GROUP = 7
WIDTH = 128
TOKENS = 256
EXTRA = 16
ROWS = 2 * TOKENS + EXTRA
AXES = ("dp", "seq")
SCALE = 1.4426950408889634 / WIDTH**0.5
LOW, HIGH = 1e-25, 1e30
VMEM_LIMIT = 16 * 1024 * 1024
NT = (((1,), (1,)), ((), ()))
NN = (((1,), (0,)), ((), ()))


def rank_of(plane, y, x):
    return (plane * 4 + y) * 4 + x


def turned_along_x(value, steps):
    pairs = [
        (rank_of(plane, y, x), rank_of(plane, y, (x + steps) % 4))
        for plane in range(16)
        for y in range(4)
        for x in range(4)
    ]
    return lax.ppermute(value, AXES, pairs)


def turned_along_y(value, steps):
    pairs = [
        (rank_of(plane, y, x), rank_of(plane, (y + steps) % 4, x))
        for plane in range(16)
        for y in range(4)
        for x in range(4)
    ]
    return lax.ppermute(value, AXES, pairs)


def two_rows_on(value):
    pairs = [
        (rank_of(plane, (y - 1) % 4, x), (rank_of(plane, y, x) + 8) % 256)
        for plane in range(16)
        for y in range(4)
        for x in range(4)
    ]
    return lax.ppermute(value, AXES, pairs)


def rows_on(value, rows):
    return lax.ppermute(value, AXES, [(r, (r + 4 * rows) % 256) for r in range(256)])


def ids_down(rows):
    halves = [
        jnp.transpose(jnp.broadcast_to(rows[i : i + 1], (WIDTH, WIDTH))) for i in range(2)
    ]
    return jnp.concatenate(halves, axis=0)


def ids_across(rows, count):
    halves = [jnp.broadcast_to(rows[i : i + 1], (count, WIDTH)) for i in range(2)]
    return jnp.concatenate(halves, axis=1)


def ids_of(block):
    return block[2 * TOKENS : ROWS, :].astype(jnp.float32)[0:2]


def general(whole, chosen, q_ref, o_ref, out, held, top, total, mix, sem):
    count = len(whole) + 1

    @pl.loop(0, KEY_VALUE_HEADS)
    def _(head):
        keys = pl.ds(pl.multiple_of(head * WIDTH, WIDTH), WIDTH)
        held[count - 2] = chosen[:, keys]
        for b, place in enumerate([*range(count - 2), count - 1]):
            held[place] = whole[b][:, keys]
        mine = ids_down(ids_of(held[count - 1]))
        mine = jnp.concatenate([mine, mine], axis=1)
        later = lax.broadcasted_iota(jnp.int32, (TOKENS, TOKENS), 1) > lax.broadcasted_iota(
            jnp.int32, (TOKENS, TOKENS), 0
        )

        @pl.loop(0, GROUP)
        def _(g):
            columns = pl.ds(pl.multiple_of((head * GROUP + g) * WIDTH, WIDTH), WIDTH)
            top[...] = jnp.full((TOKENS, WIDTH), -1e30, jnp.float32)
            total[...] = jnp.zeros((TOKENS, WIDTH), jnp.float32)
            mix[...] = jnp.zeros((TOKENS, WIDTH), jnp.float32)

            @pl.loop(0, count)
            def _(b):
                s = lax.dot_general(
                    q_ref[:, columns],
                    held[b, 0:TOKENS, :],
                    NT,
                    preferred_element_type=jnp.float32,
                )
                s = s * SCALE
                theirs = held[b, 2 * TOKENS : ROWS, :].astype(jnp.float32)[0:2]
                allowed = (mine == ids_across(theirs, TOKENS)) & ~(later & (b == count - 1))
                s = jnp.where(allowed, s, -1e30)
                now = jnp.maximum(top[:, 0:1], jnp.max(s, axis=1, keepdims=True))
                p = jnp.where(allowed, jnp.exp2(s - now), 0.0)
                keep = jnp.exp2(top[:, 0:1] - now)
                total[...] = total[...] * keep + jnp.sum(p, axis=1, keepdims=True)
                mix[...] = mix[...] * keep + lax.dot_general(
                    p.astype(jnp.bfloat16),
                    held[b, TOKENS : 2 * TOKENS, :],
                    NN,
                    preferred_element_type=jnp.float32,
                )
                top[...] = jnp.broadcast_to(now, (TOKENS, WIDTH))

            out[:, columns] = (mix[...] / total[...]).astype(jnp.bfloat16)

    copy = pltpu.make_async_copy(out, o_ref, sem)
    copy.start()
    copy.wait()


def attend(prior, has_own, has_before, last, whole_count, *refs):
    refs = list(refs)
    take = lambda n: [refs.pop(0) for _ in range(n)]
    which = take(1)[0] if last else None
    q_ref, own = take(2)
    blocks = take(prior)
    before = take(2) if has_before else None
    whole = take(whole_count)
    outs = take(1 if last else 3)
    mixed, picked, causal, rows_in = take(4)
    if last:
        chosen, out, sems = take(3)
        latter = blocks.pop()
        chosen[...] = jnp.where(which[0] == 1, latter[...], blocks[-1][...])
        blocks[-1] = chosen
        prior -= 1

    ids = ids_of(own[:, 0:WIDTH])
    down = ids_down(ids)
    first = ids[0:1, 0:1]
    rows_in[...] = jnp.where(down == first, 1.0, 0.0)
    if has_own:
        down = jnp.concatenate([down, down], axis=1)
        row = lax.broadcasted_iota(jnp.int32, (TOKENS, TOKENS), 0)
        column = lax.broadcasted_iota(jnp.int32, (TOKENS, TOKENS), 1)
        same = down == ids_across(ids, TOKENS)
        causal[...] = jnp.where(same & (column <= row), 1.0, 0.0)
    for b in range(prior):
        theirs = ids_of(blocks[b][:, 0:WIDTH])
        picked[b] = ids_down(jnp.where(theirs == first, 1.0, 0.0)).astype(jnp.bfloat16)

    def term(q, keys, b, mask=None):
        s = lax.dot_general(q, keys, NT, preferred_element_type=jnp.float32)
        p = jnp.exp2(s * SCALE)
        if mask is not None:
            p = p * mask
        return lax.dot_general(
            p.astype(jnp.bfloat16), mixed[b], NN, preferred_element_type=jnp.float32
        )

    good = None
    copies = []
    lane = lax.broadcasted_iota(jnp.int32, (TOKENS, WIDTH), 1)
    for head in range(KEY_VALUE_HEADS):
        keys = slice(head * WIDTH, (head + 1) * WIDTH)
        for b in range(prior):
            mixed[b, :, 0:WIDTH] = blocks[b][TOKENS : 2 * TOKENS, keys] * picked[b]
            mixed[b, :, WIDTH:] = picked[b]
        if has_own:
            mixed[prior, :, 0:WIDTH] = own[TOKENS : 2 * TOKENS, keys]
            mixed[prior, :, WIDTH:] = jnp.ones((TOKENS, WIDTH), jnp.bfloat16)
        weights = None
        for g in range(GROUP):
            columns = slice((head * GROUP + g) * WIDTH, (head * GROUP + g + 1) * WIDTH)
            q = q_ref[:, columns]
            mix, weight = 0.0, 0.0
            if prior:
                sums = term(q, blocks[0][0:TOKENS, keys], 0)
                for b in range(1, prior):
                    sums = sums + term(q, blocks[b][0:TOKENS, keys], b)
                inside = rows_in[...] > 0.5
                mix = jnp.where(inside, sums[:, :WIDTH], 0.0)
                weight = jnp.where(inside, sums[:, WIDTH:], 0.0)
            if has_own:
                sums = term(q, own[0:TOKENS, keys], prior, causal[...])
                mix = mix + sums[:, :WIDTH]
                weight = weight + sums[:, WIDTH:]
            if has_before:
                mix = mix + before[0][:, columns]
                weight = weight + before[1][:, head * WIDTH + g : head * WIDTH + g + 1]
            if last:
                out[:, columns] = (mix / weight).astype(jnp.bfloat16)
                fine = jnp.where((weight > LOW) & (weight < HIGH), 1.0, 0.0)
                good = fine if good is None else jnp.minimum(good, fine)
            else:
                outs[0][:, columns] = mix
                weights = weight if weights is None else jnp.where(lane == g, weight, weights)
        if last:
            columns = slice(head * GROUP * WIDTH, (head + 1) * GROUP * WIDTH)
            copy = pltpu.make_async_copy(
                out.at[:, columns], outs[0].at[:, columns], sems.at[head]
            )
            copy.start()
            copies.append(copy)
        else:
            outs[1][:, keys] = weights
    if last:
        for copy in copies:
            copy.wait()

        @pl.when(jnp.min(good) < 0.5)
        def _():
            general(whole, chosen, q_ref, outs[0], out, *refs, sems.at[0])
    else:
        outs[2][...] = jnp.zeros_like(outs[2])


def attention(queries, own, blocks, has_own, before, whole, which):
    last = which is not None
    count = len(blocks) + has_own - last
    inside = pl.BlockSpec(memory_space=pltpu.VMEM)
    if last:
        out_specs = pl.BlockSpec(memory_space=pl.ANY)
        out_shape = jax.ShapeDtypeStruct(queries.shape, jnp.bfloat16)
    else:
        out_specs = [inside] * 3
        out_shape = [
            jax.ShapeDtypeStruct(queries.shape, jnp.float32),
            jax.ShapeDtypeStruct((TOKENS, KEY_VALUE_HEADS * WIDTH), jnp.float32),
            jax.ShapeDtypeStruct((8, WIDTH), jnp.float32),
        ]
    scratch = [
        pltpu.VMEM((count, TOKENS, 2 * WIDTH), jnp.bfloat16),
        pltpu.VMEM((max(len(blocks), 1), TOKENS, WIDTH), jnp.bfloat16),
        pltpu.VMEM((TOKENS, TOKENS), jnp.float32),
        pltpu.VMEM((TOKENS, WIDTH), jnp.float32),
    ]
    if last:
        scratch += [
            pltpu.VMEM((ROWS, KEY_VALUE_HEADS * WIDTH), jnp.bfloat16),
            pltpu.VMEM(queries.shape, jnp.bfloat16),
            pltpu.SemaphoreType.DMA((KEY_VALUE_HEADS,)),
            pltpu.VMEM((len(whole) + 1, ROWS, WIDTH), jnp.bfloat16),
            pltpu.VMEM((TOKENS, WIDTH), jnp.float32),
            pltpu.VMEM((TOKENS, WIDTH), jnp.float32),
            pltpu.VMEM((TOKENS, WIDTH), jnp.float32),
        ]
    return pl.pallas_call(
        functools.partial(attend, len(blocks), has_own, bool(before), last, len(whole)),
        in_specs=[pl.BlockSpec(memory_space=pltpu.SMEM)] * last
        + [inside] * (2 + len(blocks) + len(before) + len(whole)),
        out_specs=out_specs,
        out_shape=out_shape,
        scratch_shapes=scratch,
        compiler_params=pltpu.CompilerParams(vmem_limit_bytes=VMEM_LIMIT),
        cost_estimate=pl.CostEstimate(
            flops=28 * 256 * 256 * count * 1024,
            bytes_accessed=4_000_000 + count * 540_000,
            transcendentals=28 * 256 * 256 * count,
        ),
    )(*([which.astype(jnp.int32)] if last else []), queries, own, *blocks, *before, *whole)


def per_device(queries, key_states, value_vectors, segment_ids):
    ids = segment_ids.astype(jnp.bfloat16).reshape(2, WIDTH)
    ids = jnp.pad(jnp.tile(ids, (1, KEY_VALUE_HEADS)), ((0, EXTRA - 2), (0, 0)))
    own = jnp.concatenate([key_states, value_vectors, ids], axis=0)
    x = lax.axis_index("seq") % 4
    own = lax.optimization_barrier(own)
    four = rows_on(own, 1)
    back = turned_along_y(own, -1)
    across = turned_along_x(own, 2)
    middle = [turned_along_x(four, a) for a in (1, 3)]
    eight = two_rows_on(back)
    next_across = rows_on(across, 1)
    *stage, done = attention(queries, own, [four], True, [], [], None)
    eight, across, _ = lax.optimization_barrier((eight, across, done))
    far_across = rows_on(across, 2)
    ends = [turned_along_x(jnp.where(x + a < 4, own, eight), a) for a in (1, 3)]
    early = [*middle, next_across, eight]
    *stage, _ = attention(queries, own, early, False, stage, [], None)
    late = [*ends, across, far_across]
    whole = [four, *early, *ends, own]
    return attention(queries, own, late, False, stage, whole, jnp.reshape(x < 2, (1,)))


def solution(mesh):
    rows = P(AXES, None)
    return jax.shard_map(
        per_device,
        mesh=mesh,
        in_specs=(rows, rows, rows, P(AXES)),
        out_specs=rows,
        check_vma=False,
    )
```

```python
import dataclasses
import functools

import jax
import jax.numpy as jnp
from jax import lax
from jax.experimental import pallas as pl
from jax.experimental.pallas import tpu as pltpu
from jax.sharding import PartitionSpec as P

KEY_VALUE_HEADS = 4
GROUP = 7
WIDTH = 128
TOKENS = 256
EXTRA = 16
ROWS = 2 * TOKENS + EXTRA
AXES = ("dp", "seq")
SCALE = 1.4426950408889634 / WIDTH**0.5
LOW, HIGH = 1e-25, 1e30
VMEM_LIMIT = 16 * 1024 * 1024
COST = 512
NT = (((1,), (1,)), ((), ()))
NN = (((1,), (0,)), ((), ()))


def rank_of(plane, y, x):
    return (plane * 4 + y) * 4 + x


def turned_along_x(value, steps):
    pairs = [
        (rank_of(plane, y, x), rank_of(plane, y, (x + steps) % 4))
        for plane in range(16)
        for y in range(4)
        for x in range(4)
    ]
    return lax.ppermute(value, AXES, pairs)


def turned_along_y(value, steps):
    pairs = [
        (rank_of(plane, y, x), rank_of(plane, (y + steps) % 4, x))
        for plane in range(16)
        for y in range(4)
        for x in range(4)
    ]
    return lax.ppermute(value, AXES, pairs)


def two_rows_on(value):
    pairs = [
        (rank_of(plane, (y - 1) % 4, x), (rank_of(plane, y, x) + 8) % 256)
        for plane in range(16)
        for y in range(4)
        for x in range(4)
    ]
    return lax.ppermute(value, AXES, pairs)


def rows_on(value, rows):
    return lax.ppermute(value, AXES, [(r, (r + 4 * rows) % 256) for r in range(256)])


def ids_down(rows):
    halves = [
        jnp.transpose(jnp.broadcast_to(rows[i : i + 1], (WIDTH, WIDTH))) for i in range(2)
    ]
    return jnp.concatenate(halves, axis=0)


def ids_across(rows, count):
    halves = [jnp.broadcast_to(rows[i : i + 1], (count, WIDTH)) for i in range(2)]
    return jnp.concatenate(halves, axis=1)


def ids_of(block):
    return block[2 * TOKENS : ROWS, :].astype(jnp.float32)[0:2]


def general(whole, chosen, q_ref, o_ref, out, held, top, total, mix, sem):
    count = len(whole) + 1

    @pl.loop(0, KEY_VALUE_HEADS)
    def _(head):
        keys = pl.ds(pl.multiple_of(head * WIDTH, WIDTH), WIDTH)
        held[count - 2] = chosen[:, keys]
        for b, place in enumerate([*range(count - 2), count - 1]):
            if len(whole[b]) == 1:
                held[place] = whole[b][0][:, keys]
                continue
            for part in range(2):

                @pl.when(head // 2 == part)
                def _():
                    there = pl.ds(pl.multiple_of((head - 2 * part) * WIDTH, WIDTH), WIDTH)
                    held[place] = whole[b][part][:, there]
        mine = ids_down(ids_of(held[count - 1]))
        mine = jnp.concatenate([mine, mine], axis=1)
        later = lax.broadcasted_iota(jnp.int32, (TOKENS, TOKENS), 1) > lax.broadcasted_iota(
            jnp.int32, (TOKENS, TOKENS), 0
        )

        @pl.loop(0, GROUP)
        def _(g):
            columns = pl.ds(pl.multiple_of((head * GROUP + g) * WIDTH, WIDTH), WIDTH)
            top[...] = jnp.full((TOKENS, WIDTH), -1e30, jnp.float32)
            total[...] = jnp.zeros((TOKENS, WIDTH), jnp.float32)
            mix[...] = jnp.zeros((TOKENS, WIDTH), jnp.float32)

            @pl.loop(0, count)
            def _(b):
                s = lax.dot_general(
                    q_ref[:, columns],
                    held[b, 0:TOKENS, :],
                    NT,
                    preferred_element_type=jnp.float32,
                )
                s = s * SCALE
                theirs = held[b, 2 * TOKENS : ROWS, :].astype(jnp.float32)[0:2]
                allowed = (mine == ids_across(theirs, TOKENS)) & ~(later & (b == count - 1))
                s = jnp.where(allowed, s, -1e30)
                now = jnp.maximum(top[:, 0:1], jnp.max(s, axis=1, keepdims=True))
                p = jnp.where(allowed, jnp.exp2(s - now), 0.0)
                keep = jnp.exp2(top[:, 0:1] - now)
                total[...] = total[...] * keep + jnp.sum(p, axis=1, keepdims=True)
                mix[...] = mix[...] * keep + lax.dot_general(
                    p.astype(jnp.bfloat16),
                    held[b, TOKENS : 2 * TOKENS, :],
                    NN,
                    preferred_element_type=jnp.float32,
                )
                top[...] = jnp.broadcast_to(now, (TOKENS, WIDTH))

            out[:, columns] = (mix[...] / total[...]).astype(jnp.bfloat16)

    copy = pltpu.make_async_copy(out, o_ref, sem)
    copy.start()
    copy.wait()


def attend(stage, *refs):
    refs = list(refs)
    take = lambda n: [refs.pop(0) for _ in range(n)]
    last, has_own = stage.last, stage.has_own
    which = take(1)[0] if last else None
    q_ref, own = take(2)
    blocks = list(zip(take(len(stage.heads)), stage.heads))
    before = [(*take(2), heads) for heads in stage.before]
    whole = [take(n) for n in stage.whole]
    outs = take(1 if last else 3)
    mixed, picked, causal, rows_in = take(4)
    if last:
        chosen, out, sems = take(3)
        latter, _ = blocks.pop()
        former, heads = blocks.pop()
        chosen[...] = jnp.where(which[0] == 1, latter[...], former[...])
        blocks.append((chosen, heads))

    ids = ids_of(own[:, 0:WIDTH])
    down = ids_down(ids)
    first = ids[0:1, 0:1]
    rows_in[...] = jnp.where(down == first, 1.0, 0.0)
    if has_own:
        down = jnp.concatenate([down, down], axis=1)
        row = lax.broadcasted_iota(jnp.int32, (TOKENS, TOKENS), 0)
        column = lax.broadcasted_iota(jnp.int32, (TOKENS, TOKENS), 1)
        same = down == ids_across(ids, TOKENS)
        causal[...] = jnp.where(same & (column <= row), 1.0, 0.0)
    for b, (block, _) in enumerate(blocks):
        theirs = ids_of(block[:, 0:WIDTH])
        picked[b] = ids_down(jnp.where(theirs == first, 1.0, 0.0)).astype(jnp.bfloat16)

    def term(q, keys, b, mask=None):
        s = lax.dot_general(q, keys, NT, preferred_element_type=jnp.float32)
        p = jnp.exp2(s * SCALE)
        if mask is not None:
            p = p * mask
        return lax.dot_general(
            p.astype(jnp.bfloat16), mixed[b], NN, preferred_element_type=jnp.float32
        )

    good = None
    copies = []
    lane = lax.broadcasted_iota(jnp.int32, (TOKENS, WIDTH), 1)
    for head in stage.out_heads:
        here = []
        for b, (block, heads) in enumerate(blocks):
            if head in heads:
                keys = slice(heads.index(head) * WIDTH, (heads.index(head) + 1) * WIDTH)
                mixed[b, :, 0:WIDTH] = block[TOKENS : 2 * TOKENS, keys] * picked[b]
                mixed[b, :, WIDTH:] = picked[b]
                here.append((b, block, keys))
        if has_own:
            own_keys = slice(head * WIDTH, (head + 1) * WIDTH)
            mixed[len(blocks), :, 0:WIDTH] = own[TOKENS : 2 * TOKENS, own_keys]
            mixed[len(blocks), :, WIDTH:] = jnp.ones((TOKENS, WIDTH), jnp.bfloat16)
        place = stage.out_heads.index(head)
        weights = None
        for g in range(GROUP):
            column = (head * GROUP + g) * WIDTH
            q = q_ref[:, column : column + WIDTH]
            sums = None
            for b, block, keys in here:
                t = term(q, block[0:TOKENS, keys], b)
                sums = t if sums is None else sums + t
            inside = rows_in[...] > 0.5
            mix = jnp.where(inside, sums[:, :WIDTH], 0.0)
            weight = jnp.where(inside, sums[:, WIDTH:], 0.0)
            if has_own:
                sums = term(q, own[0:TOKENS, own_keys], len(blocks), causal[...])
                mix = mix + sums[:, :WIDTH]
                weight = weight + sums[:, WIDTH:]
            for wide, narrow, heads in before:
                if head in heads:
                    i = heads.index(head)
                    at = (i * GROUP + g) * WIDTH
                    mix = mix + wide[:, at : at + WIDTH]
                    weight = weight + narrow[:, i * WIDTH + g : i * WIDTH + g + 1]
            if last:
                out[:, column : column + WIDTH] = (mix / weight).astype(jnp.bfloat16)
                fine = jnp.where((weight > LOW) & (weight < HIGH), 1.0, 0.0)
                good = fine if good is None else jnp.minimum(good, fine)
            else:
                at = (place * GROUP + g) * WIDTH
                outs[0][:, at : at + WIDTH] = mix
                weights = weight if weights is None else jnp.where(lane == g, weight, weights)
        if last:
            columns = slice(head * GROUP * WIDTH, (head + 1) * GROUP * WIDTH)
            copy = pltpu.make_async_copy(
                out.at[:, columns], outs[0].at[:, columns], sems.at[head]
            )
            copy.start()
            copies.append(copy)
        else:
            outs[1][:, place * WIDTH : (place + 1) * WIDTH] = weights
    if last:
        bad = jnp.min(good) < 0.5
        for copy in copies:
            copy.wait()

        @pl.when(bad)
        def _():
            general(whole, chosen, q_ref, outs[0], out, *refs, sems.at[0])
    else:
        outs[2][...] = jnp.zeros_like(outs[2])


ALL, LOW_HEADS, HIGH_HEADS = (0, 1, 2, 3), (0, 1), (2, 3)
NOT_LOW = (None, None, 2, 3)


@dataclasses.dataclass(frozen=True)
class Stage:
    heads: tuple
    before: tuple = ()
    out_heads: tuple = ALL
    has_own: bool = False
    cost: int = COST
    last: bool = False
    whole: tuple = ()


def attention(stage, queries, own, blocks, before=(), whole=(), which=None):
    last = stage.last
    count = len(blocks) + stage.has_own - last
    tiles = sum(len(set(heads) & set(stage.out_heads)) for heads in stage.heads[: count + last])
    inside = pl.BlockSpec(memory_space=pltpu.VMEM)
    if last:
        out_specs = pl.BlockSpec(memory_space=pl.ANY)
        out_shape = jax.ShapeDtypeStruct(queries.shape, jnp.bfloat16)
    else:
        out_specs = [inside] * 3
        n = len(stage.out_heads)
        out_shape = [
            jax.ShapeDtypeStruct((TOKENS, n * GROUP * WIDTH), jnp.float32),
            jax.ShapeDtypeStruct((TOKENS, n * WIDTH), jnp.float32),
            jax.ShapeDtypeStruct((8, WIDTH), jnp.float32),
        ]
    scratch = [
        pltpu.VMEM((count, TOKENS, 2 * WIDTH), jnp.bfloat16),
        pltpu.VMEM((len(blocks), TOKENS, WIDTH), jnp.bfloat16),
        pltpu.VMEM((TOKENS, TOKENS), jnp.float32),
        pltpu.VMEM((TOKENS, WIDTH), jnp.float32),
    ]
    if last:
        scratch += [
            pltpu.VMEM((ROWS, KEY_VALUE_HEADS * WIDTH), jnp.bfloat16),
            pltpu.VMEM(queries.shape, jnp.bfloat16),
            pltpu.SemaphoreType.DMA((KEY_VALUE_HEADS,)),
            pltpu.VMEM((len(whole) + 1, ROWS, WIDTH), jnp.bfloat16),
            pltpu.VMEM((TOKENS, WIDTH), jnp.float32),
            pltpu.VMEM((TOKENS, WIDTH), jnp.float32),
            pltpu.VMEM((TOKENS, WIDTH), jnp.float32),
        ]
    stage = dataclasses.replace(stage, whole=tuple(len(parts) for parts in whole))
    operands = [queries, own, *blocks]
    operands += [array for sums in before for array in sums]
    operands += [array for parts in whole for array in parts]
    return pl.pallas_call(
        functools.partial(attend, stage),
        in_specs=[pl.BlockSpec(memory_space=pltpu.SMEM)] * last + [inside] * len(operands),
        out_specs=out_specs,
        out_shape=out_shape,
        scratch_shapes=scratch,
        compiler_params=pltpu.CompilerParams(vmem_limit_bytes=VMEM_LIMIT),
        cost_estimate=pl.CostEstimate(
            flops=7 * 256 * 256 * (tiles + 4 * stage.has_own) * stage.cost,
            bytes_accessed=4_000_000 + count * 540_000,
            transcendentals=28 * 256 * 256 * count,
        ),
    )(*([which.astype(jnp.int32)] if last else []), *operands)


def per_device(queries, key_states, value_vectors, segment_ids):
    ids = segment_ids.astype(jnp.bfloat16).reshape(2, WIDTH)
    ids = jnp.pad(jnp.tile(ids, (1, KEY_VALUE_HEADS)), ((0, EXTRA - 2), (0, 0)))
    own = jnp.concatenate([key_states, value_vectors, ids], axis=0)
    x = lax.axis_index("seq") % 4
    own = lax.optimization_barrier(own)
    four = rows_on(own, 1)
    back = turned_along_y(own, -1)
    across = turned_along_x(own, 2)
    middle = [turned_along_x(four, a) for a in (1, 3)]
    eight = two_rows_on(back)
    next_across = rows_on(across, 1)
    *sums, done = attention(Stage((ALL,), has_own=True, cost=2048), queries, own, [four])
    eight, across, _ = lax.optimization_barrier((eight, across, done))
    far_across = rows_on(across, 2)
    low, high = [
        [
            turned_along_x(jnp.where(x + a < 4, own[:, columns], eight[:, columns]), a)
            for a in (1, 3)
        ]
        for columns in (slice(0, 2 * WIDTH), slice(2 * WIDTH, 4 * WIDTH))
    ]
    early = [*middle, next_across, eight]
    *sums, _ = attention(Stage((ALL,) * 4, before=(ALL,)), queries, own, early, [sums])
    *low_sums, _ = attention(
        Stage((LOW_HEADS,) * 2, before=(ALL,), out_heads=LOW_HEADS), queries, own, low, [sums]
    )
    return attention(
        Stage((HIGH_HEADS, HIGH_HEADS, ALL, ALL), before=(NOT_LOW, LOW_HEADS), last=True),
        queries,
        own,
        [*high, across, far_across],
        [sums, low_sums],
        [*[(block,) for block in [four, *early]], *zip(low, high), (own,)],
        jnp.reshape(x < 2, (1,)),
    )


def solution(mesh):
    rows = P(AXES, None)
    return jax.shard_map(
        per_device,
        mesh=mesh,
        in_specs=(rows, rows, rows, P(AXES)),
        out_specs=rows,
        check_vma=False,
    )
```

```python
import functools

import jax
import jax.numpy as jnp
from jax import lax
from jax.experimental import pallas as pl
from jax.experimental.pallas import tpu as pltpu
from jax.sharding import PartitionSpec as P

KEY_VALUE_HEADS = 4
GROUP = 7
WIDTH = 128
TOKENS = 256
EXTRA = 16
ROWS = 2 * TOKENS + EXTRA
AXES = ("dp", "seq")
SCALE = 1.4426950408889634 / WIDTH**0.5
LOW, HIGH = 1e-25, 1e30
VMEM_LIMIT = 20 * 1024 * 1024
NT = (((1,), (1,)), ((), ()))
NN = (((1,), (0,)), ((), ()))


def rank_of(plane, y, x):
    return (plane * 4 + y) * 4 + x


def turned_along_x(value, steps):
    pairs = [
        (rank_of(plane, y, x), rank_of(plane, y, (x + steps) % 4))
        for plane in range(16)
        for y in range(4)
        for x in range(4)
    ]
    return lax.ppermute(value, AXES, pairs)


def turned_along_y(value, steps):
    pairs = [
        (rank_of(plane, y, x), rank_of(plane, (y + steps) % 4, x))
        for plane in range(16)
        for y in range(4)
        for x in range(4)
    ]
    return lax.ppermute(value, AXES, pairs)


def two_rows_on(value):
    pairs = [
        (rank_of(plane, (y - 1) % 4, x), (rank_of(plane, y, x) + 8) % 256)
        for plane in range(16)
        for y in range(4)
        for x in range(4)
    ]
    return lax.ppermute(value, AXES, pairs)


def rows_on(value, rows):
    return lax.ppermute(value, AXES, [(r, (r + 4 * rows) % 256) for r in range(256)])


def ids_down(rows):
    halves = [
        jnp.transpose(jnp.broadcast_to(rows[i : i + 1], (WIDTH, WIDTH))) for i in range(2)
    ]
    return jnp.concatenate(halves, axis=0)


def ids_across(rows, count):
    halves = [jnp.broadcast_to(rows[i : i + 1], (count, WIDTH)) for i in range(2)]
    return jnp.concatenate(halves, axis=1)


def ids_of(block):
    return block[2 * TOKENS : ROWS, :].astype(jnp.float32)[0:2]


def general(whole, chosen, q_ref, o_ref, out, held, top, total, mix, sem):
    count = len(whole) + 1

    @pl.loop(0, KEY_VALUE_HEADS)
    def _(head):
        keys = pl.ds(pl.multiple_of(head * WIDTH, WIDTH), WIDTH)
        held[count - 2] = chosen[:, keys]
        for b, place in enumerate([*range(count - 2), count - 1]):
            held[place] = whole[b][:, keys]
        mine = ids_down(ids_of(held[count - 1]))
        mine = jnp.concatenate([mine, mine], axis=1)
        later = lax.broadcasted_iota(jnp.int32, (TOKENS, TOKENS), 1) > lax.broadcasted_iota(
            jnp.int32, (TOKENS, TOKENS), 0
        )

        @pl.loop(0, GROUP)
        def _(g):
            columns = pl.ds(pl.multiple_of((head * GROUP + g) * WIDTH, WIDTH), WIDTH)
            top[...] = jnp.full((TOKENS, WIDTH), -1e30, jnp.float32)
            total[...] = jnp.zeros((TOKENS, WIDTH), jnp.float32)
            mix[...] = jnp.zeros((TOKENS, WIDTH), jnp.float32)

            @pl.loop(0, count)
            def _(b):
                s = lax.dot_general(
                    q_ref[:, columns],
                    held[b, 0:TOKENS, :],
                    NT,
                    preferred_element_type=jnp.float32,
                )
                s = s * SCALE
                theirs = held[b, 2 * TOKENS : ROWS, :].astype(jnp.float32)[0:2]
                allowed = (mine == ids_across(theirs, TOKENS)) & ~(later & (b == count - 1))
                s = jnp.where(allowed, s, -1e30)
                now = jnp.maximum(top[:, 0:1], jnp.max(s, axis=1, keepdims=True))
                p = jnp.where(allowed, jnp.exp2(s - now), 0.0)
                keep = jnp.exp2(top[:, 0:1] - now)
                total[...] = total[...] * keep + jnp.sum(p, axis=1, keepdims=True)
                mix[...] = mix[...] * keep + lax.dot_general(
                    p.astype(jnp.bfloat16),
                    held[b, TOKENS : 2 * TOKENS, :],
                    NN,
                    preferred_element_type=jnp.float32,
                )
                top[...] = jnp.broadcast_to(now, (TOKENS, WIDTH))

            out[:, columns] = (mix[...] / total[...]).astype(jnp.bfloat16)

    copy = pltpu.make_async_copy(out, o_ref, sem)
    copy.start()
    copy.wait()


def attend(prior, has_own, has_before, last, whole_count, *refs):
    refs = list(refs)
    take = lambda n: [refs.pop(0) for _ in range(n)]
    which = take(1)[0] if last else None
    q_ref, own = take(2)
    blocks = take(prior)
    before = take(2) if has_before else None
    whole = take(whole_count)
    outs = take(1 if last else 3)
    mixed, picked, causal, rows_in = take(4)
    if last:
        chosen, out, sems, total, narrow = take(5)
        latter = blocks.pop()
        chosen[...] = jnp.where(which[0] == 1, latter[...], blocks[-1][...])
        blocks[-1] = chosen
        prior -= 1
    else:
        total, narrow = outs[0], outs[1]

    ids = ids_of(own[:, 0:WIDTH])
    down = ids_down(ids)
    first = ids[0:1, 0:1]
    rows_in[...] = jnp.where(down == first, 1.0, 0.0)
    lane = lax.broadcasted_iota(jnp.int32, (TOKENS, WIDTH), 1)
    hits = [
        jnp.where(ids_of(block[:, 0:WIDTH]) == first, 1.0, 0.0) for block in blocks
    ]

    def term(q, keys, values, mask=None):
        s = lax.dot_general(q, keys, NT, preferred_element_type=jnp.float32)
        p = jnp.exp2(s * SCALE)
        if mask is not None:
            p = p * mask
        return lax.dot_general(
            p.astype(jnp.bfloat16), values[...], NN, preferred_element_type=jnp.float32
        )

    def pick(b):
        picked[b] = ids_down(hits[b]).astype(jnp.bfloat16)

    def mix_in(b, keys):
        mixed[b, :, 0:WIDTH] = blocks[b][TOKENS : 2 * TOKENS, keys] * picked[b]
        mixed[b, :, WIDTH:] = picked[b]

    def masked_term(b, q, keys):
        t = term(q, blocks[b][0:TOKENS, keys], mixed.at[b])
        inside = rows_in[...] > 0.5
        return jnp.where(inside, t[:, :WIDTH], 0.0), jnp.where(inside, t[:, WIDTH:], 0.0)

    def heads():
        for head in range(KEY_VALUE_HEADS):
            keys = slice(head * WIDTH, (head + 1) * WIDTH)
            columns = [
                slice((head * GROUP + g) * WIDTH, (head * GROUP + g + 1) * WIDTH)
                for g in range(GROUP)
            ]
            yield head, keys, columns

    def add(b, wide_from, narrow_from):
        pick(b)
        for head, keys, columns in heads():
            mix_in(b, keys)
            weights = narrow_from[:, keys]
            for g in range(GROUP):
                mix, weight = masked_term(b, q_ref[:, columns[g]], keys)
                total[:, columns[g]] = wide_from[:, columns[g]] + mix
                weights = weights + jnp.where(lane == g, weight, 0.0)
            narrow[:, keys] = weights

    def finish(b):
        good = None
        if b is not None:
            pick(b)
        for head, keys, columns in heads():
            if b is not None:
                mix_in(b, keys)
            for g in range(GROUP):
                mix = total[:, columns[g]]
                weight = jnp.broadcast_to(
                    narrow[:, head * WIDTH + g : head * WIDTH + g + 1], (TOKENS, WIDTH)
                )
                if b is not None:
                    more, extra = masked_term(b, q_ref[:, columns[g]], keys)
                    mix, weight = mix + more, weight + extra
                out[:, columns[g]] = (mix / weight).astype(jnp.bfloat16)
                fine = jnp.where((weight > LOW) & (weight < HIGH), 1.0, 0.0)
                good = fine if good is None else jnp.minimum(good, fine)
            at = slice(columns[0].start, columns[-1].stop)
            pltpu.make_async_copy(out.at[:, at], outs[0].at[:, at], sems.at[head]).start()
        rows_in[...] = good

    if has_own:
        down = jnp.concatenate([down, down], axis=1)
        row = lax.broadcasted_iota(jnp.int32, (TOKENS, TOKENS), 0)
        column = lax.broadcasted_iota(jnp.int32, (TOKENS, TOKENS), 1)
        same = down == ids_across(ids, TOKENS)
        causal[...] = jnp.where(same & (column <= row), 1.0, 0.0)
        for b in range(prior):
            pick(b)
        for head, keys, columns in heads():
            mixed[prior, :, 0:WIDTH] = own[TOKENS : 2 * TOKENS, keys]
            mixed[prior, :, WIDTH:] = jnp.ones((TOKENS, WIDTH), jnp.bfloat16)
            for b in range(prior):
                mix_in(b, keys)
            weights = jnp.zeros((TOKENS, WIDTH), jnp.float32)
            for g in range(GROUP):
                q = q_ref[:, columns[g]]
                t = term(q, own[0:TOKENS, keys], mixed.at[prior], causal[...])
                mix, weight = t[:, :WIDTH], t[:, WIDTH:]
                for b in range(prior):
                    more, extra = masked_term(b, q, keys)
                    mix, weight = mix + more, weight + extra
                total[:, columns[g]] = mix
                weights = jnp.where(lane == g, weight, weights)
            narrow[:, keys] = weights
        outs[2][...] = jnp.zeros_like(outs[2])
        return

    needed = [jnp.max(hit) > 0.5 for hit in hits]

    @pl.when(needed[0])
    def _():
        add(0, *before)

    @pl.when(~needed[0])
    def _():
        total[...] = before[0][...]
        narrow[...] = before[1][...]

    for b in range(1, prior - last):

        @pl.when(needed[b])
        def _(b=b):
            add(b, total, narrow)

    if not last:
        outs[2][...] = jnp.zeros_like(outs[2])
        return

    @pl.when(needed[-1])
    def _():
        finish(prior - 1)

    @pl.when(~needed[-1])
    def _():
        finish(None)

    bad = jnp.min(rows_in[...]) < 0.5
    for head, keys, columns in heads():
        at = slice(columns[0].start, columns[-1].stop)
        pltpu.make_async_copy(out.at[:, at], outs[0].at[:, at], sems.at[head]).wait()

    @pl.when(bad)
    def _():
        general(whole, chosen, q_ref, outs[0], out, *refs, sems.at[0])


def attention(queries, own, blocks, has_own, before, whole, which):
    last = which is not None
    count = len(blocks) + has_own - last
    inside = pl.BlockSpec(memory_space=pltpu.VMEM)
    if last:
        out_specs = pl.BlockSpec(memory_space=pl.ANY)
        out_shape = jax.ShapeDtypeStruct(queries.shape, jnp.bfloat16)
    else:
        out_specs = [inside] * 3
        out_shape = [
            jax.ShapeDtypeStruct(queries.shape, jnp.float32),
            jax.ShapeDtypeStruct((TOKENS, KEY_VALUE_HEADS * WIDTH), jnp.float32),
            jax.ShapeDtypeStruct((8, WIDTH), jnp.float32),
        ]
    scratch = [
        pltpu.VMEM((count, TOKENS, 2 * WIDTH), jnp.bfloat16),
        pltpu.VMEM((max(len(blocks), 1), TOKENS, WIDTH), jnp.bfloat16),
        pltpu.VMEM((TOKENS, TOKENS), jnp.float32),
        pltpu.VMEM((TOKENS, WIDTH), jnp.float32),
    ]
    if last:
        scratch += [
            pltpu.VMEM((ROWS, KEY_VALUE_HEADS * WIDTH), jnp.bfloat16),
            pltpu.VMEM(queries.shape, jnp.bfloat16),
            pltpu.SemaphoreType.DMA((KEY_VALUE_HEADS,)),
            pltpu.VMEM(queries.shape, jnp.float32),
            pltpu.VMEM((TOKENS, KEY_VALUE_HEADS * WIDTH), jnp.float32),
            pltpu.VMEM((len(whole) + 1, ROWS, WIDTH), jnp.bfloat16),
            pltpu.VMEM((TOKENS, WIDTH), jnp.float32),
            pltpu.VMEM((TOKENS, WIDTH), jnp.float32),
            pltpu.VMEM((TOKENS, WIDTH), jnp.float32),
        ]
    return pl.pallas_call(
        functools.partial(attend, len(blocks), has_own, bool(before), last, len(whole)),
        in_specs=[pl.BlockSpec(memory_space=pltpu.SMEM)] * last
        + [inside] * (2 + len(blocks) + len(before) + len(whole)),
        out_specs=out_specs,
        out_shape=out_shape,
        scratch_shapes=scratch,
        compiler_params=pltpu.CompilerParams(vmem_limit_bytes=VMEM_LIMIT),
        cost_estimate=pl.CostEstimate(
            flops=28 * 256 * 256 * count * 1024,
            bytes_accessed=4_000_000 + count * 540_000,
            transcendentals=28 * 256 * 256 * count,
        ),
    )(*([which.astype(jnp.int32)] if last else []), queries, own, *blocks, *before, *whole)


def per_device(queries, key_states, value_vectors, segment_ids):
    ids = segment_ids.astype(jnp.bfloat16).reshape(2, WIDTH)
    ids = jnp.pad(jnp.tile(ids, (1, KEY_VALUE_HEADS)), ((0, EXTRA - 2), (0, 0)))
    own = jnp.concatenate([key_states, value_vectors, ids], axis=0)
    x = lax.axis_index("seq") % 4
    own = lax.optimization_barrier(own)
    four = rows_on(own, 1)
    back = turned_along_y(own, -1)
    across = turned_along_x(own, 2)
    middle = [turned_along_x(four, a) for a in (1, 3)]
    eight = two_rows_on(back)
    next_across = rows_on(across, 1)
    *stage, done = attention(queries, own, [four], True, [], [], None)
    eight, across, _ = lax.optimization_barrier((eight, across, done))
    far_across = rows_on(across, 2)
    ends = [turned_along_x(jnp.where(x + a < 4, own, eight), a) for a in (1, 3)]
    early = [*middle, next_across, eight]
    *stage, _ = attention(queries, own, early, False, stage, [], None)
    late = [*ends, across, far_across]
    whole = [four, *early, *ends, own]
    return attention(queries, own, late, False, stage, whole, jnp.reshape(x < 2, (1,)))


def solution(mesh):
    rows = P(AXES, None)
    return jax.shard_map(
        per_device,
        mesh=mesh,
        in_specs=(rows, rows, rows, P(AXES)),
        out_specs=rows,
        check_vma=False,
    )
```

```python
import functools

import jax
import jax.numpy as jnp
from jax import lax
from jax.experimental import pallas as pl
from jax.experimental.pallas import tpu as pltpu
from jax.sharding import PartitionSpec as P

KEY_VALUE_HEADS = 4
GROUP = 7
WIDTH = 128
TOKENS = 256
EXTRA = 16
ROWS = 2 * TOKENS + EXTRA
AXES = ("dp", "seq")
SCALE = 1.4426950408889634 / WIDTH**0.5
LOW, HIGH = 1e-25, 1e30
VMEM_LIMIT = 16 * 1024 * 1024
COST = 1024
NT = (((1,), (1,)), ((), ()))
NN = (((1,), (0,)), ((), ()))


def rank_of(plane, y, x):
    return (plane * 4 + y) * 4 + x


def turned_along_x(value, steps):
    pairs = [
        (rank_of(plane, y, x), rank_of(plane, y, (x + steps) % 4))
        for plane in range(16)
        for y in range(4)
        for x in range(4)
    ]
    return lax.ppermute(value, AXES, pairs)


def turned_along_y(value, steps):
    pairs = [
        (rank_of(plane, y, x), rank_of(plane, (y + steps) % 4, x))
        for plane in range(16)
        for y in range(4)
        for x in range(4)
    ]
    return lax.ppermute(value, AXES, pairs)


def two_rows_on(value):
    pairs = [
        (rank_of(plane, (y - 1) % 4, x), (rank_of(plane, y, x) + 8) % 256)
        for plane in range(16)
        for y in range(4)
        for x in range(4)
    ]
    return lax.ppermute(value, AXES, pairs)


def rows_on(value, rows):
    return lax.ppermute(value, AXES, [(r, (r + 4 * rows) % 256) for r in range(256)])


def ids_down(rows):
    halves = [
        jnp.transpose(jnp.broadcast_to(rows[i : i + 1], (WIDTH, WIDTH))) for i in range(2)
    ]
    return jnp.concatenate(halves, axis=0)


def ids_across(rows, count):
    halves = [jnp.broadcast_to(rows[i : i + 1], (count, WIDTH)) for i in range(2)]
    return jnp.concatenate(halves, axis=1)


def ids_of(block):
    return block[2 * TOKENS : ROWS, :].astype(jnp.float32)[0:2]


def general(whole, which, q_ref, o_ref, out, held, top, total, mix, sem):
    *whole, former, latter = whole
    count = len(whole) + 1

    @pl.loop(0, KEY_VALUE_HEADS)
    def _(head):
        keys = pl.ds(pl.multiple_of(head * WIDTH, WIDTH), WIDTH)
        held[count - 2] = jnp.where(which[0] == 1, latter[:, keys], former[:, keys])
        for b, place in enumerate([*range(count - 2), count - 1]):
            held[place] = whole[b][:, keys]
        mine = ids_down(ids_of(held[count - 1]))
        mine = jnp.concatenate([mine, mine], axis=1)
        later = lax.broadcasted_iota(jnp.int32, (TOKENS, TOKENS), 1) > lax.broadcasted_iota(
            jnp.int32, (TOKENS, TOKENS), 0
        )

        @pl.loop(0, GROUP)
        def _(g):
            columns = pl.ds(pl.multiple_of((head * GROUP + g) * WIDTH, WIDTH), WIDTH)
            top[...] = jnp.full((TOKENS, WIDTH), -1e30, jnp.float32)
            total[...] = jnp.zeros((TOKENS, WIDTH), jnp.float32)
            mix[...] = jnp.zeros((TOKENS, WIDTH), jnp.float32)

            @pl.loop(0, count)
            def _(b):
                s = lax.dot_general(
                    q_ref[:, columns],
                    held[b, 0:TOKENS, :],
                    NT,
                    preferred_element_type=jnp.float32,
                )
                s = s * SCALE
                theirs = held[b, 2 * TOKENS : ROWS, :].astype(jnp.float32)[0:2]
                allowed = (mine == ids_across(theirs, TOKENS)) & ~(later & (b == count - 1))
                s = jnp.where(allowed, s, -1e30)
                now = jnp.maximum(top[:, 0:1], jnp.max(s, axis=1, keepdims=True))
                p = jnp.where(allowed, jnp.exp2(s - now), 0.0)
                keep = jnp.exp2(top[:, 0:1] - now)
                total[...] = total[...] * keep + jnp.sum(p, axis=1, keepdims=True)
                mix[...] = mix[...] * keep + lax.dot_general(
                    p.astype(jnp.bfloat16),
                    held[b, TOKENS : 2 * TOKENS, :],
                    NN,
                    preferred_element_type=jnp.float32,
                )
                top[...] = jnp.broadcast_to(now, (TOKENS, WIDTH))

            out[:, columns] = (mix[...] / total[...]).astype(jnp.bfloat16)

    copy = pltpu.make_async_copy(out, o_ref, sem)
    copy.start()
    copy.wait()


def attend(prior, has_own, has_before, last, whole_count, gated, which, *refs):
    refs = list(refs)
    take = lambda n: [refs.pop(0) for _ in range(n)]
    q_ref, own = take(2)
    blocks = take(prior)
    before = take(2) if has_before else None
    whole = take(whole_count)
    outs = take(1 if last else 2)
    mixed, picked, causal, rows_in = take(4)
    if last:
        out, sems = take(2)
    else:
        total, narrow = outs

    ids = ids_of(own[:, 0:WIDTH])
    down = ids_down(ids)
    first = ids[0:1, 0:1]
    rows_in[...] = jnp.where(down == first, 1.0, 0.0)
    lane = lax.broadcasted_iota(jnp.int32, (TOKENS, WIDTH), 1)
    hits = [
        jnp.where(ids_of(block[:, 0:WIDTH]) == first, 1.0, 0.0) for block in blocks
    ]

    def term(q, keys, values, mask=None):
        s = lax.dot_general(q, keys, NT, preferred_element_type=jnp.float32)
        p = jnp.exp2(s * SCALE)
        if mask is not None:
            p = p * mask
        return lax.dot_general(
            p.astype(jnp.bfloat16), values[...], NN, preferred_element_type=jnp.float32
        )

    def pick(b):
        picked[b] = ids_down(hits[b]).astype(jnp.bfloat16)

    def mix_in(b, keys):
        mixed[b, :, 0:WIDTH] = blocks[b][TOKENS : 2 * TOKENS, keys] * picked[b]
        mixed[b, :, WIDTH:] = picked[b]

    def masked_term(b, q, keys):
        t = term(q, blocks[b][0:TOKENS, keys], mixed.at[b])
        inside = rows_in[...] > 0.5
        return jnp.where(inside, t[:, :WIDTH], 0.0), jnp.where(inside, t[:, WIDTH:], 0.0)

    def heads():
        for head in range(KEY_VALUE_HEADS):
            keys = slice(head * WIDTH, (head + 1) * WIDTH)
            columns = [
                slice((head * GROUP + g) * WIDTH, (head * GROUP + g + 1) * WIDTH)
                for g in range(GROUP)
            ]
            yield head, keys, columns

    def add(b, wide_from, narrow_from):
        pick(b)
        for head, keys, columns in heads():
            mix_in(b, keys)
            weights = narrow_from[:, keys]
            for g in range(GROUP):
                mix, weight = masked_term(b, q_ref[:, columns[g]], keys)
                total[:, columns[g]] = wide_from[:, columns[g]] + mix
                weights = weights + jnp.where(lane == g, weight, 0.0)
            narrow[:, keys] = weights

    def finish(b):
        good = None
        if b is not None:
            pick(b)
        for head, keys, columns in heads():
            if b is not None:
                mix_in(b, keys)
            for g in range(GROUP):
                mix = before[0][:, columns[g]]
                weight = jnp.broadcast_to(
                    before[1][:, head * WIDTH + g : head * WIDTH + g + 1], (TOKENS, WIDTH)
                )
                if b is not None:
                    more, extra = masked_term(b, q_ref[:, columns[g]], keys)
                    mix, weight = mix + more, weight + extra
                out[:, columns[g]] = (mix / weight).astype(jnp.bfloat16)
                fine = jnp.where((weight > LOW) & (weight < HIGH), 1.0, 0.0)
                good = fine if good is None else jnp.minimum(good, fine)
            at = slice(columns[0].start, columns[-1].stop)
            pltpu.make_async_copy(out.at[:, at], outs[0].at[:, at], sems.at[head]).start()
        rows_in[...] = good

    needed = [jnp.max(hit) > 0.5 for hit in hits]
    for b, flag in gated:
        needed[b] = needed[b] & (which[0] == flag)

    if last:

        @pl.when(needed[0])
        def _():
            finish(0)

        @pl.when(~needed[0])
        def _():
            finish(None)

    elif has_own:
        down = jnp.concatenate([down, down], axis=1)
        row = lax.broadcasted_iota(jnp.int32, (TOKENS, TOKENS), 0)
        column = lax.broadcasted_iota(jnp.int32, (TOKENS, TOKENS), 1)
        same = down == ids_across(ids, TOKENS)
        causal[...] = jnp.where(same & (column <= row), 1.0, 0.0)
        for head, keys, columns in heads():
            mixed[prior, :, 0:WIDTH] = own[TOKENS : 2 * TOKENS, keys]
            mixed[prior, :, WIDTH:] = jnp.ones((TOKENS, WIDTH), jnp.bfloat16)
            weights = jnp.zeros((TOKENS, WIDTH), jnp.float32)
            for g in range(GROUP):
                q = q_ref[:, columns[g]]
                t = term(q, own[0:TOKENS, keys], mixed.at[prior], causal[...])
                total[:, columns[g]] = t[:, :WIDTH]
                weights = jnp.where(lane == g, t[:, WIDTH:], weights)
            narrow[:, keys] = weights
    else:

        @pl.when(needed[0])
        def _():
            add(0, *before)

        @pl.when(~needed[0])
        def _():
            total[...] = before[0][...]
            narrow[...] = before[1][...]

    if not last:
        for b in range(0 if has_own else 1, prior):

            @pl.when(needed[b])
            def _(b=b):
                add(b, total, narrow)

        return

    bad = jnp.min(rows_in[...]) < 0.5
    for head, keys, columns in heads():
        at = slice(columns[0].start, columns[-1].stop)
        pltpu.make_async_copy(out.at[:, at], outs[0].at[:, at], sems.at[head]).wait()

    @pl.when(bad)
    def _():
        general(whole, which, q_ref, outs[0], out, *refs, sems.at[0])


def attention(which, queries, own, blocks, has_own=False, before=(), whole=(), gated=()):
    last = bool(whole)
    count = len(blocks) + has_own
    inside = pl.BlockSpec(memory_space=pltpu.VMEM)
    if last:
        out_specs = pl.BlockSpec(memory_space=pl.ANY)
        out_shape = jax.ShapeDtypeStruct(queries.shape, jnp.bfloat16)
    else:
        out_specs = [inside] * 2
        out_shape = [
            jax.ShapeDtypeStruct(queries.shape, jnp.float32),
            jax.ShapeDtypeStruct((TOKENS, KEY_VALUE_HEADS * WIDTH), jnp.float32),
        ]
    scratch = [
        pltpu.VMEM((count, TOKENS, 2 * WIDTH), jnp.bfloat16),
        pltpu.VMEM((len(blocks), TOKENS, WIDTH), jnp.bfloat16),
        pltpu.VMEM((TOKENS, TOKENS), jnp.float32),
        pltpu.VMEM((TOKENS, WIDTH), jnp.float32),
    ]
    if last:
        scratch += [
            pltpu.VMEM(queries.shape, jnp.bfloat16),
            pltpu.SemaphoreType.DMA((KEY_VALUE_HEADS,)),
            pltpu.VMEM((len(whole) - 1, ROWS, WIDTH), jnp.bfloat16),
            pltpu.VMEM((TOKENS, WIDTH), jnp.float32),
            pltpu.VMEM((TOKENS, WIDTH), jnp.float32),
            pltpu.VMEM((TOKENS, WIDTH), jnp.float32),
        ]
    operands = [queries, own, *blocks, *before, *whole]
    return pl.pallas_call(
        functools.partial(
            attend, len(blocks), has_own, bool(before), last, len(whole), tuple(gated)
        ),
        in_specs=[pl.BlockSpec(memory_space=pltpu.SMEM)] + [inside] * len(operands),
        out_specs=out_specs,
        out_shape=out_shape,
        scratch_shapes=scratch,
        compiler_params=pltpu.CompilerParams(vmem_limit_bytes=VMEM_LIMIT),
        cost_estimate=pl.CostEstimate(
            flops=28 * 256 * 256 * count * COST,
            bytes_accessed=4_000_000 + count * 540_000,
            transcendentals=28 * 256 * 256 * count,
        ),
    )(which, *operands)


def per_device(queries, key_states, value_vectors, segment_ids):
    ids = segment_ids.astype(jnp.bfloat16).reshape(2, WIDTH)
    ids = jnp.pad(jnp.tile(ids, (1, KEY_VALUE_HEADS)), ((0, EXTRA - 2), (0, 0)))
    own = jnp.concatenate([key_states, value_vectors, ids], axis=0)
    x = lax.axis_index("seq") % 4
    own = lax.optimization_barrier(own)
    four = rows_on(own, 1)
    back = turned_along_y(own, -1)
    across = turned_along_x(own, 2)
    middle = [turned_along_x(four, a) for a in (1, 3)]
    eight = two_rows_on(back)
    next_across = rows_on(across, 1)
    far_across = rows_on(across, 2)
    ends = [turned_along_x(jnp.where(x + a < 4, own, eight), a) for a in (1, 3)]
    early = [*middle, next_across, eight]
    which = jnp.reshape(x < 2, (1,)).astype(jnp.int32)
    attend_to = functools.partial(attention, which, queries, own)
    sums = attend_to([four, across], has_own=True, gated=[(1, 0)])
    sums = attend_to(early, before=sums)
    sums = attend_to(ends, before=sums)
    whole = [four, *early, *ends, own, across, far_across]
    return attend_to([far_across], before=sums, gated=[(0, 1)], whole=whole)


def solution(mesh):
    rows = P(AXES, None)
    return jax.shard_map(
        per_device,
        mesh=mesh,
        in_specs=(rows, rows, rows, P(AXES)),
        out_specs=rows,
        check_vma=False,
    )
```

```python
import functools

import jax
import jax.numpy as jnp
from jax import lax
from jax.experimental import pallas as pl
from jax.experimental.pallas import tpu as pltpu
from jax.sharding import PartitionSpec as P

KEY_VALUE_HEADS = 4
GROUP = 7
WIDTH = 128
TOKENS = 256
EXTRA = 16
ROWS = 2 * TOKENS + EXTRA
AXES = ("dp", "seq")
SCALE = 1.4426950408889634 / WIDTH**0.5
LOW, HIGH = 1e-25, 1e30
VMEM_LIMIT = 16 * 1024 * 1024
COST = 1024
NT = (((1,), (1,)), ((), ()))
NN = (((1,), (0,)), ((), ()))


def rank_of(plane, y, x):
    return (plane * 4 + y) * 4 + x


def turned_along_x(value, steps):
    pairs = [
        (rank_of(plane, y, x), rank_of(plane, y, (x + steps) % 4))
        for plane in range(16)
        for y in range(4)
        for x in range(4)
    ]
    return lax.ppermute(value, AXES, pairs)


def turned_along_y(value, steps):
    pairs = [
        (rank_of(plane, y, x), rank_of(plane, (y + steps) % 4, x))
        for plane in range(16)
        for y in range(4)
        for x in range(4)
    ]
    return lax.ppermute(value, AXES, pairs)


def two_rows_on(value):
    pairs = [
        (rank_of(plane, (y - 1) % 4, x), (rank_of(plane, y, x) + 8) % 256)
        for plane in range(16)
        for y in range(4)
        for x in range(4)
    ]
    return lax.ppermute(value, AXES, pairs)


def rows_on(value, rows):
    return lax.ppermute(value, AXES, [(r, (r + 4 * rows) % 256) for r in range(256)])


def ids_down(rows):
    halves = [
        jnp.transpose(jnp.broadcast_to(rows[i : i + 1], (WIDTH, WIDTH))) for i in range(2)
    ]
    return jnp.concatenate(halves, axis=0)


def ids_across(rows, count):
    halves = [jnp.broadcast_to(rows[i : i + 1], (count, WIDTH)) for i in range(2)]
    return jnp.concatenate(halves, axis=1)


def ids_of(block):
    return block[2 * TOKENS : ROWS, :].astype(jnp.float32)[0:2]


def general(whole, which, q_ref, o_ref, out, held, top, total, mix, sem):
    *whole, former, latter = whole
    count = len(whole) + 1

    @pl.loop(0, KEY_VALUE_HEADS)
    def _(head):
        keys = pl.ds(pl.multiple_of(head * WIDTH, WIDTH), WIDTH)
        held[count - 2] = jnp.where(which[0] == 1, latter[:, keys], former[:, keys])
        for b, place in enumerate([*range(count - 2), count - 1]):
            held[place] = whole[b][:, keys]
        mine = ids_down(ids_of(held[count - 1]))
        mine = jnp.concatenate([mine, mine], axis=1)
        later = lax.broadcasted_iota(jnp.int32, (TOKENS, TOKENS), 1) > lax.broadcasted_iota(
            jnp.int32, (TOKENS, TOKENS), 0
        )

        @pl.loop(0, GROUP)
        def _(g):
            columns = pl.ds(pl.multiple_of((head * GROUP + g) * WIDTH, WIDTH), WIDTH)
            top[...] = jnp.full((TOKENS, WIDTH), -1e30, jnp.float32)
            total[...] = jnp.zeros((TOKENS, WIDTH), jnp.float32)
            mix[...] = jnp.zeros((TOKENS, WIDTH), jnp.float32)

            @pl.loop(0, count)
            def _(b):
                s = lax.dot_general(
                    q_ref[:, columns],
                    held[b, 0:TOKENS, :],
                    NT,
                    preferred_element_type=jnp.float32,
                )
                s = s * SCALE
                theirs = held[b, 2 * TOKENS : ROWS, :].astype(jnp.float32)[0:2]
                allowed = (mine == ids_across(theirs, TOKENS)) & ~(later & (b == count - 1))
                s = jnp.where(allowed, s, -1e30)
                now = jnp.maximum(top[:, 0:1], jnp.max(s, axis=1, keepdims=True))
                p = jnp.where(allowed, jnp.exp2(s - now), 0.0)
                keep = jnp.exp2(top[:, 0:1] - now)
                total[...] = total[...] * keep + jnp.sum(p, axis=1, keepdims=True)
                mix[...] = mix[...] * keep + lax.dot_general(
                    p.astype(jnp.bfloat16),
                    held[b, TOKENS : 2 * TOKENS, :],
                    NN,
                    preferred_element_type=jnp.float32,
                )
                top[...] = jnp.broadcast_to(now, (TOKENS, WIDTH))

            out[:, columns] = (mix[...] / total[...]).astype(jnp.bfloat16)

    copy = pltpu.make_async_copy(out, o_ref, sem)
    copy.start()
    copy.wait()


def attend(prior, has_own, has_before, last, whole_count, gated, which, *refs):
    refs = list(refs)
    take = lambda n: [refs.pop(0) for _ in range(n)]
    q_ref, own = take(2)
    blocks = take(prior)
    before = take(2) if has_before else None
    whole = take(whole_count)
    outs = take(1 if last else 2)
    mixed, picked, causal, rows_in = take(4)
    if last:
        out, sems = take(2)
    else:
        total, narrow = outs

    ids = ids_of(own[:, 0:WIDTH])
    down = ids_down(ids)
    first = ids[0:1, 0:1]
    rows_in[...] = jnp.where(down == first, 1.0, 0.0)
    lane = lax.broadcasted_iota(jnp.int32, (TOKENS, WIDTH), 1)
    hits = [
        jnp.where(ids_of(block[:, 0:WIDTH]) == first, 1.0, 0.0) for block in blocks
    ]

    def term(q, keys, values, mask=None):
        s = lax.dot_general(q, keys, NT, preferred_element_type=jnp.float32)
        p = jnp.exp2(s * SCALE)
        if mask is not None:
            p = p * mask
        return lax.dot_general(
            p.astype(jnp.bfloat16), values[...], NN, preferred_element_type=jnp.float32
        )

    def pick(b):
        picked[b] = ids_down(hits[b]).astype(jnp.bfloat16)

    def mix_in(b, keys):
        mixed[b, :, 0:WIDTH] = blocks[b][TOKENS : 2 * TOKENS, keys] * picked[b]
        mixed[b, :, WIDTH:] = picked[b]

    def masked_term(b, q, keys):
        t = term(q, blocks[b][0:TOKENS, keys], mixed.at[b])
        inside = rows_in[...] > 0.5
        return jnp.where(inside, t[:, :WIDTH], 0.0), jnp.where(inside, t[:, WIDTH:], 0.0)

    def heads():
        for head in range(KEY_VALUE_HEADS):
            keys = slice(head * WIDTH, (head + 1) * WIDTH)
            columns = [
                slice((head * GROUP + g) * WIDTH, (head * GROUP + g + 1) * WIDTH)
                for g in range(GROUP)
            ]
            yield head, keys, columns

    def add(b, wide_from, narrow_from):
        pick(b)
        for head, keys, columns in heads():
            mix_in(b, keys)
            weights = narrow_from[:, keys]
            for g in range(GROUP):
                mix, weight = masked_term(b, q_ref[:, columns[g]], keys)
                total[:, columns[g]] = wide_from[:, columns[g]] + mix
                weights = weights + jnp.where(lane == g, weight, 0.0)
            narrow[:, keys] = weights

    def finish(b):
        good = None
        if b is not None:
            pick(b)
        for head, keys, columns in heads():
            if b is not None:
                mix_in(b, keys)
            for g in range(GROUP):
                mix = before[0][:, columns[g]]
                weight = jnp.broadcast_to(
                    before[1][:, head * WIDTH + g : head * WIDTH + g + 1], (TOKENS, WIDTH)
                )
                if b is not None:
                    more, extra = masked_term(b, q_ref[:, columns[g]], keys)
                    mix, weight = mix + more, weight + extra
                out[:, columns[g]] = (mix / weight).astype(jnp.bfloat16)
                fine = jnp.where((weight > LOW) & (weight < HIGH), 1.0, 0.0)
                good = fine if good is None else jnp.minimum(good, fine)
            at = slice(columns[0].start, columns[-1].stop)
            pltpu.make_async_copy(out.at[:, at], outs[0].at[:, at], sems.at[head]).start()
        rows_in[...] = good

    needed = [jnp.max(hit) > 0.5 for hit in hits]
    for b, flag in gated:
        needed[b] = needed[b] & (which[0] == flag)

    if last:

        @pl.when(needed[0])
        def _():
            finish(0)

        @pl.when(~needed[0])
        def _():
            finish(None)

    elif has_own:
        down = jnp.concatenate([down, down], axis=1)
        row = lax.broadcasted_iota(jnp.int32, (TOKENS, TOKENS), 0)
        column = lax.broadcasted_iota(jnp.int32, (TOKENS, TOKENS), 1)
        same = down == ids_across(ids, TOKENS)
        causal[...] = jnp.where(same & (column <= row), 1.0, 0.0)
        for head, keys, columns in heads():
            mixed[prior, :, 0:WIDTH] = own[TOKENS : 2 * TOKENS, keys]
            mixed[prior, :, WIDTH:] = jnp.ones((TOKENS, WIDTH), jnp.bfloat16)
            weights = jnp.zeros((TOKENS, WIDTH), jnp.float32)
            for g in range(GROUP):
                q = q_ref[:, columns[g]]
                t = term(q, own[0:TOKENS, keys], mixed.at[prior], causal[...])
                total[:, columns[g]] = t[:, :WIDTH]
                weights = jnp.where(lane == g, t[:, WIDTH:], weights)
            narrow[:, keys] = weights
    else:

        @pl.when(needed[0])
        def _():
            add(0, *before)

        @pl.when(~needed[0])
        def _():
            total[...] = before[0][...]
            narrow[...] = before[1][...]

    if not last:
        for b in range(0 if has_own else 1, prior):

            @pl.when(needed[b])
            def _(b=b):
                add(b, total, narrow)

        return

    bad = jnp.min(rows_in[...]) < 0.5
    for head, keys, columns in heads():
        at = slice(columns[0].start, columns[-1].stop)
        pltpu.make_async_copy(out.at[:, at], outs[0].at[:, at], sems.at[head]).wait()

    @pl.when(bad)
    def _():
        general(whole, which, q_ref, outs[0], out, *refs, sems.at[0])


def attention(which, queries, own, blocks, has_own=False, before=(), whole=(), gated=()):
    last = bool(whole)
    count = len(blocks) + has_own
    inside = pl.BlockSpec(memory_space=pltpu.VMEM)
    if last:
        out_specs = pl.BlockSpec(memory_space=pl.ANY)
        out_shape = jax.ShapeDtypeStruct(queries.shape, jnp.bfloat16)
    else:
        out_specs = [inside] * 2
        out_shape = [
            jax.ShapeDtypeStruct(queries.shape, jnp.float32),
            jax.ShapeDtypeStruct((TOKENS, KEY_VALUE_HEADS * WIDTH), jnp.float32),
        ]
    scratch = [
        pltpu.VMEM((count, TOKENS, 2 * WIDTH), jnp.bfloat16),
        pltpu.VMEM((len(blocks), TOKENS, WIDTH), jnp.bfloat16),
        pltpu.VMEM((TOKENS, TOKENS), jnp.float32),
        pltpu.VMEM((TOKENS, WIDTH), jnp.float32),
    ]
    if last:
        scratch += [
            pltpu.VMEM(queries.shape, jnp.bfloat16),
            pltpu.SemaphoreType.DMA((KEY_VALUE_HEADS,)),
            pltpu.VMEM((len(whole) - 1, ROWS, WIDTH), jnp.bfloat16),
            pltpu.VMEM((TOKENS, WIDTH), jnp.float32),
            pltpu.VMEM((TOKENS, WIDTH), jnp.float32),
            pltpu.VMEM((TOKENS, WIDTH), jnp.float32),
        ]
    operands = [queries, own, *blocks, *before, *whole]
    return pl.pallas_call(
        functools.partial(
            attend, len(blocks), has_own, bool(before), last, len(whole), tuple(gated)
        ),
        in_specs=[pl.BlockSpec(memory_space=pltpu.SMEM)] + [inside] * len(operands),
        out_specs=out_specs,
        out_shape=out_shape,
        scratch_shapes=scratch,
        compiler_params=pltpu.CompilerParams(vmem_limit_bytes=VMEM_LIMIT),
        cost_estimate=pl.CostEstimate(
            flops=28 * 256 * 256 * count * COST,
            bytes_accessed=4_000_000 + count * 540_000,
            transcendentals=28 * 256 * 256 * count,
        ),
    )(which, *operands)


def per_device(queries, key_states, value_vectors, segment_ids):
    ids = segment_ids.astype(jnp.bfloat16).reshape(2, WIDTH)
    ids = jnp.pad(jnp.tile(ids, (1, KEY_VALUE_HEADS)), ((0, EXTRA - 2), (0, 0)))
    own = jnp.concatenate([key_states, value_vectors, ids], axis=0)
    x = lax.axis_index("seq") % 4
    own = lax.optimization_barrier(own)
    four = rows_on(own, 1)
    back = turned_along_y(own, -1)
    across = turned_along_x(own, 2)
    middle = [turned_along_x(four, a) for a in (1, 3)]
    eight = two_rows_on(back)
    next_across = rows_on(across, 1)
    far_across = rows_on(next_across, 1)
    ends = [turned_along_x(jnp.where(x + a < 4, own, eight), a) for a in (1, 3)]
    early = [*middle, next_across, eight]
    which = jnp.reshape(x < 2, (1,)).astype(jnp.int32)
    attend_to = functools.partial(attention, which, queries, own)
    sums = attend_to([four, across], has_own=True, gated=[(1, 0)])
    sums = attend_to(early, before=sums)
    sums = attend_to(ends, before=sums)
    whole = [four, *early, *ends, own, across, far_across]
    return attend_to([far_across], before=sums, gated=[(0, 1)], whole=whole)


def solution(mesh):
    rows = P(AXES, None)
    return jax.shard_map(
        per_device,
        mesh=mesh,
        in_specs=(rows, rows, rows, P(AXES)),
        out_specs=rows,
        check_vma=False,
    )
```

```python
import functools

import jax
import jax.numpy as jnp
from jax import lax
from jax.experimental import pallas as pl
from jax.experimental.pallas import tpu as pltpu
from jax.sharding import PartitionSpec as P

KEY_VALUE_HEADS = 4
GROUP = 7
WIDTH = 128
TOKENS = 256
EXTRA = 16
ROWS = 2 * TOKENS + EXTRA
AXES = ("dp", "seq")
SCALE = 1.4426950408889634 / WIDTH**0.5
LOW, HIGH = 1e-25, 1e30
VMEM_LIMIT = 16 * 1024 * 1024
COST = 1024
NT = (((1,), (1,)), ((), ()))
NN = (((1,), (0,)), ((), ()))


def rank_of(plane, y, x):
    return (plane * 4 + y) * 4 + x


def turned_along_x(value, steps):
    pairs = [
        (rank_of(plane, y, x), rank_of(plane, y, (x + steps) % 4))
        for plane in range(16)
        for y in range(4)
        for x in range(4)
    ]
    return lax.ppermute(value, AXES, pairs)


def turned_along_y(value, steps):
    pairs = [
        (rank_of(plane, y, x), rank_of(plane, (y + steps) % 4, x))
        for plane in range(16)
        for y in range(4)
        for x in range(4)
    ]
    return lax.ppermute(value, AXES, pairs)


def two_rows_on(value):
    pairs = [
        (rank_of(plane, (y - 1) % 4, x), (rank_of(plane, y, x) + 8) % 256)
        for plane in range(16)
        for y in range(4)
        for x in range(4)
    ]
    return lax.ppermute(value, AXES, pairs)


def rows_on(value, rows):
    return lax.ppermute(value, AXES, [(r, (r + 4 * rows) % 256) for r in range(256)])


def ids_down(rows):
    halves = [
        jnp.transpose(jnp.broadcast_to(rows[i : i + 1], (WIDTH, WIDTH))) for i in range(2)
    ]
    return jnp.concatenate(halves, axis=0)


def ids_across(rows, count):
    halves = [jnp.broadcast_to(rows[i : i + 1], (count, WIDTH)) for i in range(2)]
    return jnp.concatenate(halves, axis=1)


def ids_of(block):
    return block[2 * TOKENS : ROWS, :].astype(jnp.float32)[0:2]


def general(whole, which, q_ref, o_ref, out, held, top, total, mix, sem):
    *whole, former, latter = whole
    count = len(whole) + 1

    @pl.loop(0, KEY_VALUE_HEADS)
    def _(head):
        keys = pl.ds(pl.multiple_of(head * WIDTH, WIDTH), WIDTH)
        held[count - 2] = jnp.where(which[0] == 1, latter[:, keys], former[:, keys])
        for b, place in enumerate([*range(count - 2), count - 1]):
            held[place] = whole[b][:, keys]
        mine = ids_down(ids_of(held[count - 1]))
        mine = jnp.concatenate([mine, mine], axis=1)
        later = lax.broadcasted_iota(jnp.int32, (TOKENS, TOKENS), 1) > lax.broadcasted_iota(
            jnp.int32, (TOKENS, TOKENS), 0
        )

        @pl.loop(0, GROUP)
        def _(g):
            columns = pl.ds(pl.multiple_of((head * GROUP + g) * WIDTH, WIDTH), WIDTH)
            top[...] = jnp.full((TOKENS, WIDTH), -1e30, jnp.float32)
            total[...] = jnp.zeros((TOKENS, WIDTH), jnp.float32)
            mix[...] = jnp.zeros((TOKENS, WIDTH), jnp.float32)

            @pl.loop(0, count)
            def _(b):
                s = lax.dot_general(
                    q_ref[:, columns],
                    held[b, 0:TOKENS, :],
                    NT,
                    preferred_element_type=jnp.float32,
                )
                s = s * SCALE
                theirs = held[b, 2 * TOKENS : ROWS, :].astype(jnp.float32)[0:2]
                allowed = (mine == ids_across(theirs, TOKENS)) & ~(later & (b == count - 1))
                s = jnp.where(allowed, s, -1e30)
                now = jnp.maximum(top[:, 0:1], jnp.max(s, axis=1, keepdims=True))
                p = jnp.where(allowed, jnp.exp2(s - now), 0.0)
                keep = jnp.exp2(top[:, 0:1] - now)
                total[...] = total[...] * keep + jnp.sum(p, axis=1, keepdims=True)
                mix[...] = mix[...] * keep + lax.dot_general(
                    p.astype(jnp.bfloat16),
                    held[b, TOKENS : 2 * TOKENS, :],
                    NN,
                    preferred_element_type=jnp.float32,
                )
                top[...] = jnp.broadcast_to(now, (TOKENS, WIDTH))

            out[:, columns] = (mix[...] / total[...]).astype(jnp.bfloat16)

    copy = pltpu.make_async_copy(out, o_ref, sem)
    copy.start()
    copy.wait()


def attend(prior, has_own, has_before, last, whole_count, gated, which, *refs):
    refs = list(refs)
    take = lambda n: [refs.pop(0) for _ in range(n)]
    q_ref, own = take(2)
    blocks = take(prior)
    before = take(2) if has_before else None
    whole = take(whole_count)
    outs = take(1 if last else 2)
    mixed, picked, causal, rows_in = take(4)
    if last:
        out, sems = take(2)
    else:
        total, narrow = outs

    ids = ids_of(own[:, 0:WIDTH])
    down = ids_down(ids)
    first = ids[0:1, 0:1]
    rows_in[...] = jnp.where(down == first, 1.0, 0.0)
    lane = lax.broadcasted_iota(jnp.int32, (TOKENS, WIDTH), 1)
    hits = [
        jnp.where(ids_of(block[:, 0:WIDTH]) == first, 1.0, 0.0) for block in blocks
    ]

    def term(q, keys, values, mask=None):
        s = lax.dot_general(q, keys, NT, preferred_element_type=jnp.float32)
        p = jnp.exp2(s * SCALE)
        if mask is not None:
            p = p * mask
        return lax.dot_general(
            p.astype(jnp.bfloat16), values[...], NN, preferred_element_type=jnp.float32
        )

    def pick(b):
        picked[b] = ids_down(hits[b]).astype(jnp.bfloat16)

    def mix_in(b, keys):
        mixed[b, :, 0:WIDTH] = blocks[b][TOKENS : 2 * TOKENS, keys] * picked[b]
        mixed[b, :, WIDTH:] = picked[b]

    def masked_term(b, q, keys):
        t = term(q, blocks[b][0:TOKENS, keys], mixed.at[b])
        inside = rows_in[...] > 0.5
        return jnp.where(inside, t[:, :WIDTH], 0.0), jnp.where(inside, t[:, WIDTH:], 0.0)

    def heads():
        for head in range(KEY_VALUE_HEADS):
            keys = slice(head * WIDTH, (head + 1) * WIDTH)
            columns = [
                slice((head * GROUP + g) * WIDTH, (head * GROUP + g + 1) * WIDTH)
                for g in range(GROUP)
            ]
            yield head, keys, columns

    def add(some, wide_from, narrow_from):
        for b in some:
            pick(b)
        for head, keys, columns in heads():
            for b in some:
                mix_in(b, keys)
            weights = narrow_from[:, keys]
            for g in range(GROUP):
                q = q_ref[:, columns[g]]
                sums = None
                for b in some:
                    t = term(q, blocks[b][0:TOKENS, keys], mixed.at[b])
                    sums = t if sums is None else sums + t
                inside = rows_in[...] > 0.5
                mix = jnp.where(inside, sums[:, :WIDTH], 0.0)
                total[:, columns[g]] = wide_from[:, columns[g]] + mix
                weights = weights + jnp.where(inside & (lane == g), sums[:, WIDTH:], 0.0)
            narrow[:, keys] = weights

    def send(head, columns):
        at = slice(columns[0].start, columns[-1].stop)
        return pltpu.make_async_copy(out.at[:, at], outs[0].at[:, at], sems.at[head])

    def finish():
        good = None
        for head, keys, columns in heads():
            weight = before[1][:, keys]
            fine = jnp.where((weight > LOW) & (weight < HIGH) | (lane >= GROUP), 1.0, 0.0)
            good = fine if good is None else jnp.minimum(good, fine)
            share = 1.0 / jnp.where(lane >= GROUP, 1.0, weight)
            for g in range(GROUP):
                mix = before[0][:, columns[g]] * share[:, g : g + 1]
                out[:, columns[g]] = mix.astype(jnp.bfloat16)
            send(head, columns).start()
        rows_in[...] = good

    def add_and_finish(b):
        good = None
        pick(b)
        for head, keys, columns in heads():
            mix_in(b, keys)
            for g in range(GROUP):
                more, extra = masked_term(b, q_ref[:, columns[g]], keys)
                mix = before[0][:, columns[g]] + more
                weight = extra + before[1][:, head * WIDTH + g : head * WIDTH + g + 1]
                out[:, columns[g]] = (mix / weight).astype(jnp.bfloat16)
                fine = jnp.where((weight > LOW) & (weight < HIGH), 1.0, 0.0)
                good = fine if good is None else jnp.minimum(good, fine)
            send(head, columns).start()
        rows_in[...] = good

    needed = [jnp.max(hit) > 0.5 for hit in hits]
    for b, flag in gated:
        needed[b] = needed[b] & (which[0] == flag)

    if last:

        @pl.when(needed[0])
        def _():
            add_and_finish(0)

        @pl.when(~needed[0])
        def _():
            finish()

    elif has_own:
        down = jnp.concatenate([down, down], axis=1)
        row = lax.broadcasted_iota(jnp.int32, (TOKENS, TOKENS), 0)
        column = lax.broadcasted_iota(jnp.int32, (TOKENS, TOKENS), 1)
        same = down == ids_across(ids, TOKENS)
        causal[...] = jnp.where(same & (column <= row), 1.0, 0.0)
        for head, keys, columns in heads():
            mixed[prior, :, 0:WIDTH] = own[TOKENS : 2 * TOKENS, keys]
            mixed[prior, :, WIDTH:] = jnp.ones((TOKENS, WIDTH), jnp.bfloat16)
            weights = jnp.zeros((TOKENS, WIDTH), jnp.float32)
            for g in range(GROUP):
                q = q_ref[:, columns[g]]
                t = term(q, own[0:TOKENS, keys], mixed.at[prior], causal[...])
                total[:, columns[g]] = t[:, :WIDTH]
                weights = jnp.where(lane == g, t[:, WIDTH:], weights)
            narrow[:, keys] = weights
        for b in range(prior):

            @pl.when(needed[b])
            def _(b=b):
                add([b], total, narrow)

    else:
        every = functools.reduce(jnp.logical_and, needed)

        @pl.when(every)
        def _():
            add(range(prior), *before)

        @pl.when(needed[0] & ~every)
        def _():
            add([0], *before)

        @pl.when(~needed[0])
        def _():
            total[...] = before[0][...]
            narrow[...] = before[1][...]

        for b in range(1, prior):

            @pl.when(needed[b] & ~every)
            def _(b=b):
                add([b], total, narrow)

    if not last:
        return

    bad = jnp.min(rows_in[...]) < 0.5
    for head, keys, columns in heads():
        send(head, columns).wait()

    @pl.when(bad)
    def _():
        general(whole, which, q_ref, outs[0], out, *refs, sems.at[0])


def attention(which, queries, own, blocks, has_own=False, before=(), whole=(), gated=()):
    last = bool(whole)
    count = len(blocks) + has_own
    inside = pl.BlockSpec(memory_space=pltpu.VMEM)
    if last:
        out_specs = pl.BlockSpec(memory_space=pl.ANY)
        out_shape = jax.ShapeDtypeStruct(queries.shape, jnp.bfloat16)
    else:
        out_specs = [inside] * 2
        out_shape = [
            jax.ShapeDtypeStruct(queries.shape, jnp.float32),
            jax.ShapeDtypeStruct((TOKENS, KEY_VALUE_HEADS * WIDTH), jnp.float32),
        ]
    scratch = [
        pltpu.VMEM((count, TOKENS, 2 * WIDTH), jnp.bfloat16),
        pltpu.VMEM((len(blocks), TOKENS, WIDTH), jnp.bfloat16),
        pltpu.VMEM((TOKENS, TOKENS), jnp.float32),
        pltpu.VMEM((TOKENS, WIDTH), jnp.float32),
    ]
    if last:
        scratch += [
            pltpu.VMEM(queries.shape, jnp.bfloat16),
            pltpu.SemaphoreType.DMA((KEY_VALUE_HEADS,)),
            pltpu.VMEM((len(whole) - 1, ROWS, WIDTH), jnp.bfloat16),
            pltpu.VMEM((TOKENS, WIDTH), jnp.float32),
            pltpu.VMEM((TOKENS, WIDTH), jnp.float32),
            pltpu.VMEM((TOKENS, WIDTH), jnp.float32),
        ]
    operands = [queries, own, *blocks, *before, *whole]
    return pl.pallas_call(
        functools.partial(
            attend, len(blocks), has_own, bool(before), last, len(whole), tuple(gated)
        ),
        in_specs=[pl.BlockSpec(memory_space=pltpu.SMEM)] + [inside] * len(operands),
        out_specs=out_specs,
        out_shape=out_shape,
        scratch_shapes=scratch,
        compiler_params=pltpu.CompilerParams(vmem_limit_bytes=VMEM_LIMIT),
        cost_estimate=pl.CostEstimate(
            flops=28 * 256 * 256 * count * COST,
            bytes_accessed=4_000_000 + count * 540_000,
            transcendentals=28 * 256 * 256 * count,
        ),
    )(which, *operands)


def per_device(queries, key_states, value_vectors, segment_ids):
    ids = segment_ids.astype(jnp.bfloat16).reshape(2, WIDTH)
    ids = jnp.pad(jnp.tile(ids, (1, KEY_VALUE_HEADS)), ((0, EXTRA - 2), (0, 0)))
    own = jnp.concatenate([key_states, value_vectors, ids], axis=0)
    x = lax.axis_index("seq") % 4
    own = lax.optimization_barrier(own)
    four = rows_on(own, 1)
    back = turned_along_y(own, -1)
    across = turned_along_x(own, 2)
    middle = [turned_along_x(four, a) for a in (1, 3)]
    eight = two_rows_on(back)
    next_across = rows_on(across, 1)
    far_across = rows_on(next_across, 1)
    ends = [turned_along_x(jnp.where(x + a < 4, own, eight), a) for a in (1, 3)]
    early = [*middle, next_across, eight]
    which = jnp.reshape(x < 2, (1,)).astype(jnp.int32)
    attend_to = functools.partial(attention, which, queries, own)
    sums = attend_to([four, across], has_own=True, gated=[(1, 0)])
    sums = attend_to(early, before=sums)
    sums = attend_to(ends, before=sums)
    whole = [four, *early, *ends, own, across, far_across]
    return attend_to([far_across], before=sums, gated=[(0, 1)], whole=whole)


def solution(mesh):
    rows = P(AXES, None)
    return jax.shard_map(
        per_device,
        mesh=mesh,
        in_specs=(rows, rows, rows, P(AXES)),
        out_specs=rows,
        check_vma=False,
    )
```

```python
import functools

import jax
import jax.numpy as jnp
from jax import lax
from jax.experimental import pallas as pl
from jax.experimental.pallas import tpu as pltpu
from jax.sharding import PartitionSpec as P

KEY_VALUE_HEADS = 4
GROUP = 7
WIDTH = 128
TOKENS = 256
EXTRA = 16
ROWS = 2 * TOKENS + EXTRA
AXES = ("dp", "seq")
SCALE = 1.4426950408889634 / WIDTH**0.5
LOW, HIGH = 1e-25, 1e30
VMEM_LIMIT = 16 * 1024 * 1024
COST = 1024
NT = (((1,), (1,)), ((), ()))
NN = (((1,), (0,)), ((), ()))


def rank_of(plane, y, x):
    return (plane * 4 + y) * 4 + x


def turned_along_x(value, steps):
    pairs = [
        (rank_of(plane, y, x), rank_of(plane, y, (x + steps) % 4))
        for plane in range(16)
        for y in range(4)
        for x in range(4)
    ]
    return lax.ppermute(value, AXES, pairs)


def turned_along_y(value, steps):
    pairs = [
        (rank_of(plane, y, x), rank_of(plane, (y + steps) % 4, x))
        for plane in range(16)
        for y in range(4)
        for x in range(4)
    ]
    return lax.ppermute(value, AXES, pairs)


def two_rows_on(value):
    pairs = [
        (rank_of(plane, (y - 1) % 4, x), (rank_of(plane, y, x) + 8) % 256)
        for plane in range(16)
        for y in range(4)
        for x in range(4)
    ]
    return lax.ppermute(value, AXES, pairs)


def rows_on(value, rows):
    return lax.ppermute(value, AXES, [(r, (r + 4 * rows) % 256) for r in range(256)])


def ids_down(rows):
    halves = [
        jnp.transpose(jnp.broadcast_to(rows[i : i + 1], (WIDTH, WIDTH))) for i in range(2)
    ]
    return jnp.concatenate(halves, axis=0)


def ids_across(rows, count):
    halves = [jnp.broadcast_to(rows[i : i + 1], (count, WIDTH)) for i in range(2)]
    return jnp.concatenate(halves, axis=1)


def ids_of(block):
    return block[2 * TOKENS : ROWS, :].astype(jnp.float32)[0:2]


def general(whole, which, q_ref, o_ref, out, held, top, total, mix, sem):
    *whole, former, latter = whole
    count = len(whole) + 1

    @pl.loop(0, KEY_VALUE_HEADS)
    def _(head):
        keys = pl.ds(pl.multiple_of(head * WIDTH, WIDTH), WIDTH)
        held[count - 2] = jnp.where(which[0] == 1, latter[:, keys], former[:, keys])
        for b, place in enumerate([*range(count - 2), count - 1]):
            held[place] = whole[b][:, keys]
        mine = ids_down(ids_of(held[count - 1]))
        mine = jnp.concatenate([mine, mine], axis=1)
        later = lax.broadcasted_iota(jnp.int32, (TOKENS, TOKENS), 1) > lax.broadcasted_iota(
            jnp.int32, (TOKENS, TOKENS), 0
        )

        @pl.loop(0, GROUP)
        def _(g):
            columns = pl.ds(pl.multiple_of((head * GROUP + g) * WIDTH, WIDTH), WIDTH)
            top[...] = jnp.full((TOKENS, WIDTH), -1e30, jnp.float32)
            total[...] = jnp.zeros((TOKENS, WIDTH), jnp.float32)
            mix[...] = jnp.zeros((TOKENS, WIDTH), jnp.float32)

            @pl.loop(0, count)
            def _(b):
                s = lax.dot_general(
                    q_ref[:, columns],
                    held[b, 0:TOKENS, :],
                    NT,
                    preferred_element_type=jnp.float32,
                )
                s = s * SCALE
                theirs = held[b, 2 * TOKENS : ROWS, :].astype(jnp.float32)[0:2]
                allowed = (mine == ids_across(theirs, TOKENS)) & ~(later & (b == count - 1))
                s = jnp.where(allowed, s, -1e30)
                now = jnp.maximum(top[:, 0:1], jnp.max(s, axis=1, keepdims=True))
                p = jnp.where(allowed, jnp.exp2(s - now), 0.0)
                keep = jnp.exp2(top[:, 0:1] - now)
                total[...] = total[...] * keep + jnp.sum(p, axis=1, keepdims=True)
                mix[...] = mix[...] * keep + lax.dot_general(
                    p.astype(jnp.bfloat16),
                    held[b, TOKENS : 2 * TOKENS, :],
                    NN,
                    preferred_element_type=jnp.float32,
                )
                top[...] = jnp.broadcast_to(now, (TOKENS, WIDTH))

            out[:, columns] = (mix[...] / total[...]).astype(jnp.bfloat16)

    copy = pltpu.make_async_copy(out, o_ref, sem)
    copy.start()
    copy.wait()


def attend(prior, has_own, has_before, last, whole_count, gated, which, *refs):
    refs = list(refs)
    take = lambda n: [refs.pop(0) for _ in range(n)]
    q_ref, own = take(2)
    blocks = take(prior)
    before = take(2) if has_before else None
    whole = take(whole_count)
    outs = take(1 if last else 3 if has_own else 2)
    mixed, picked, causal, rows_in = take(4)
    if last:
        out, sems = take(2)
    else:
        total, narrow = outs[:2]

    ids = ids_of(own[:, 0:WIDTH])
    down = ids_down(ids)
    first = ids[0:1, 0:1]
    rows_in[...] = jnp.where(down == first, 1.0, 0.0)
    lane = lax.broadcasted_iota(jnp.int32, (TOKENS, WIDTH), 1)
    hits = [
        jnp.where(ids_of(block[:, 0:WIDTH]) == first, 1.0, 0.0) for block in blocks
    ]

    def term(q, keys, values, mask=None):
        s = lax.dot_general(q, keys, NT, preferred_element_type=jnp.float32)
        p = jnp.exp2(s * SCALE)
        if mask is not None:
            p = p * mask
        return lax.dot_general(
            p.astype(jnp.bfloat16), values[...], NN, preferred_element_type=jnp.float32
        )

    def pick(b):
        picked[b] = ids_down(hits[b]).astype(jnp.bfloat16)

    def mix_in(b, keys):
        mixed[b, :, 0:WIDTH] = blocks[b][TOKENS : 2 * TOKENS, keys] * picked[b]
        mixed[b, :, WIDTH:] = picked[b]

    def masked_term(b, q, keys):
        t = term(q, blocks[b][0:TOKENS, keys], mixed.at[b])
        inside = rows_in[...] > 0.5
        return jnp.where(inside, t[:, :WIDTH], 0.0), jnp.where(inside, t[:, WIDTH:], 0.0)

    def heads():
        for head in range(KEY_VALUE_HEADS):
            keys = slice(head * WIDTH, (head + 1) * WIDTH)
            columns = [
                slice((head * GROUP + g) * WIDTH, (head * GROUP + g + 1) * WIDTH)
                for g in range(GROUP)
            ]
            yield head, keys, columns

    def add(b, wide_from, narrow_from):
        pick(b)
        for head, keys, columns in heads():
            mix_in(b, keys)
            weights = narrow_from[:, keys]
            for g in range(GROUP):
                mix, weight = masked_term(b, q_ref[:, columns[g]], keys)
                total[:, columns[g]] = wide_from[:, columns[g]] + mix
                weights = weights + jnp.where(lane == g, weight, 0.0)
            narrow[:, keys] = weights

    def send(head, columns):
        at = slice(columns[0].start, columns[-1].stop)
        return pltpu.make_async_copy(out.at[:, at], outs[0].at[:, at], sems.at[head])

    def finish():
        good = None
        for head, keys, columns in heads():
            weight = before[1][:, keys]
            fine = jnp.where((weight > LOW) & (weight < HIGH) | (lane >= GROUP), 1.0, 0.0)
            good = fine if good is None else jnp.minimum(good, fine)
            share = 1.0 / jnp.where(lane >= GROUP, 1.0, weight)
            for g in range(GROUP):
                mix = before[0][:, columns[g]] * share[:, g : g + 1]
                out[:, columns[g]] = mix.astype(jnp.bfloat16)
            send(head, columns).start()
        rows_in[...] = good

    def add_and_finish(b):
        good = None
        pick(b)
        for head, keys, columns in heads():
            mix_in(b, keys)
            for g in range(GROUP):
                more, extra = masked_term(b, q_ref[:, columns[g]], keys)
                mix = before[0][:, columns[g]] + more
                weight = extra + before[1][:, head * WIDTH + g : head * WIDTH + g + 1]
                out[:, columns[g]] = (mix / weight).astype(jnp.bfloat16)
                fine = jnp.where((weight > LOW) & (weight < HIGH), 1.0, 0.0)
                good = fine if good is None else jnp.minimum(good, fine)
            send(head, columns).start()
        rows_in[...] = good

    needed = [jnp.max(hit) > 0.5 for hit in hits]
    for b, flag in gated:
        needed[b] = needed[b] & (which[0] == flag)

    if last:

        @pl.when(needed[0])
        def _():
            add_and_finish(0)

        @pl.when(~needed[0])
        def _():
            finish()

    elif has_own:
        down = jnp.concatenate([down, down], axis=1)
        row = lax.broadcasted_iota(jnp.int32, (TOKENS, TOKENS), 0)
        column = lax.broadcasted_iota(jnp.int32, (TOKENS, TOKENS), 1)
        same = down == ids_across(ids, TOKENS)
        causal[...] = jnp.where(same & (column <= row), 1.0, 0.0)
        for head, keys, columns in heads():
            mixed[prior, :, 0:WIDTH] = own[TOKENS : 2 * TOKENS, keys]
            mixed[prior, :, WIDTH:] = jnp.ones((TOKENS, WIDTH), jnp.bfloat16)
            weights = jnp.zeros((TOKENS, WIDTH), jnp.float32)
            for g in range(GROUP):
                q = q_ref[:, columns[g]]
                t = term(q, own[0:TOKENS, keys], mixed.at[prior], causal[...])
                total[:, columns[g]] = t[:, :WIDTH]
                weights = jnp.where(lane == g, t[:, WIDTH:], weights)
            narrow[:, keys] = weights
        outs[2][...] = jnp.zeros_like(outs[2])
    else:

        @pl.when(needed[0])
        def _():
            add(0, *before)

        @pl.when(~needed[0])
        def _():
            total[...] = before[0][...]
            narrow[...] = before[1][...]

    if not last:
        for b in range(0 if has_own else 1, prior):

            @pl.when(needed[b])
            def _(b=b):
                add(b, total, narrow)

        return

    bad = jnp.min(rows_in[...]) < 0.5
    for head, keys, columns in heads():
        send(head, columns).wait()

    @pl.when(bad)
    def _():
        general(whole, which, q_ref, outs[0], out, *refs, sems.at[0])


def attention(which, queries, own, blocks, has_own=False, before=(), whole=(), gated=()):
    last = bool(whole)
    count = len(blocks) + has_own
    inside = pl.BlockSpec(memory_space=pltpu.VMEM)
    if last:
        out_specs = pl.BlockSpec(memory_space=pl.ANY)
        out_shape = jax.ShapeDtypeStruct(queries.shape, jnp.bfloat16)
    else:
        out_specs = [inside] * (2 + has_own)
        out_shape = [
            jax.ShapeDtypeStruct(queries.shape, jnp.float32),
            jax.ShapeDtypeStruct((TOKENS, KEY_VALUE_HEADS * WIDTH), jnp.float32),
        ] + [jax.ShapeDtypeStruct((8, WIDTH), jnp.float32)] * has_own
    scratch = [
        pltpu.VMEM((count, TOKENS, 2 * WIDTH), jnp.bfloat16),
        pltpu.VMEM((max(len(blocks), 1), TOKENS, WIDTH), jnp.bfloat16),
        pltpu.VMEM((TOKENS, TOKENS), jnp.float32),
        pltpu.VMEM((TOKENS, WIDTH), jnp.float32),
    ]
    if last:
        scratch += [
            pltpu.VMEM(queries.shape, jnp.bfloat16),
            pltpu.SemaphoreType.DMA((KEY_VALUE_HEADS,)),
            pltpu.VMEM((len(whole) - 1, ROWS, WIDTH), jnp.bfloat16),
            pltpu.VMEM((TOKENS, WIDTH), jnp.float32),
            pltpu.VMEM((TOKENS, WIDTH), jnp.float32),
            pltpu.VMEM((TOKENS, WIDTH), jnp.float32),
        ]
    operands = [queries, own, *blocks, *before, *whole]
    return pl.pallas_call(
        functools.partial(
            attend, len(blocks), has_own, bool(before), last, len(whole), tuple(gated)
        ),
        in_specs=[pl.BlockSpec(memory_space=pltpu.SMEM)] + [inside] * len(operands),
        out_specs=out_specs,
        out_shape=out_shape,
        scratch_shapes=scratch,
        compiler_params=pltpu.CompilerParams(vmem_limit_bytes=VMEM_LIMIT),
        cost_estimate=pl.CostEstimate(
            flops=28 * 256 * 256 * count * COST,
            bytes_accessed=4_000_000 + count * 540_000,
            transcendentals=28 * 256 * 256 * count,
        ),
    )(which, *operands)


def per_device(queries, key_states, value_vectors, segment_ids):
    ids = segment_ids.astype(jnp.bfloat16).reshape(2, WIDTH)
    ids = jnp.pad(jnp.tile(ids, (1, KEY_VALUE_HEADS)), ((0, EXTRA - 2), (0, 0)))
    own = jnp.concatenate([key_states, value_vectors, ids], axis=0)
    x = lax.axis_index("seq") % 4
    own = lax.optimization_barrier(own)
    four = rows_on(own, 1)
    back = turned_along_y(own, -1)
    across = turned_along_x(own, 2)
    which = jnp.reshape(x < 2, (1,)).astype(jnp.int32)
    attend_to = functools.partial(attention, which, queries, own)
    *sums, zero = attend_to([], has_own=True)
    back = jnp.where(zero[0, 0] == 0, back, own)
    middle = [turned_along_x(four, a) for a in (1, 3)]
    eight = two_rows_on(back)
    next_across = rows_on(across, 1)
    far_across = rows_on(next_across, 1)
    ends = [turned_along_x(jnp.where(x + a < 4, own, eight), a) for a in (1, 3)]
    early = [*middle, next_across, eight]
    sums = attend_to([four, across], before=sums, gated=[(1, 0)])
    sums = attend_to(early, before=sums)
    sums = attend_to(ends, before=sums)
    whole = [four, *early, *ends, own, across, far_across]
    return attend_to([far_across], before=sums, gated=[(0, 1)], whole=whole)


def solution(mesh):
    rows = P(AXES, None)
    return jax.shard_map(
        per_device,
        mesh=mesh,
        in_specs=(rows, rows, rows, P(AXES)),
        out_specs=rows,
        check_vma=False,
    )
```
